32 devices in a mesh: seq: 16 (over z, y, x), head: 2 (over core).
Axes of the slice: x: 2, y: 2, z: 4, core: 2. Of those that a mesh axis runs over, the one named last changes fastest.
Arguments:
- layer_input: bfloat16 [2, 8192, 1792], P(None, 'seq', 'head'), may hold values from -6 to 6
- cotangent: bfloat16 [2, 8192, 1792], P(None, 'seq', 'head'), may hold values from -6 to 6
- lengths: int32 [2, 4], replicated, may hold values from 1 to 7808, as said below
- doc_order: int32 [2, 4], replicated, may hold values from 0 to 3, as said below
- norm_gains: bfloat16 [2, 1792], P(None, 'seq'), may hold values from 0.5 to 1.5
- conv_filter: bfloat16 [3, 1792], P(None, 'seq'), may hold values from -3 to 3
- w_query: bfloat16 [1792, 256], P('seq', 'head'), may hold values from -0.125 to 0.125
- w_key: bfloat16 [1792, 256], P('seq', 'head'), may hold values from -0.125 to 0.125
- w_value: bfloat16 [1792, 1792], P('seq', 'head'), may hold values from -0.125 to 0.125
- w_wquery: bfloat16 [1792, 1792], P('seq', 'head'), may hold values from -0.125 to 0.125
- w_wkey: bfloat16 [1792, 1792], P('seq', 'head'), may hold values from -0.125 to 0.125
- w_conv_in: bfloat16 [1792, 1792], P('seq', 'head'), may hold values from -0.125 to 0.125
- w_conv_gate: bfloat16 [1792, 1792], P('seq', 'head'), may hold values from -0.125 to 0.125
- w_out: bfloat16 [1792, 1792], P('head', 'seq'), may hold values from -0.1875 to 0.1875
- w_gate: bfloat16 [1792, 4864], P('seq', 'head'), may hold values from -0.125 to 0.125
- w_up: bfloat16 [1792, 4864], P('seq', 'head'), may hold values from -0.125 to 0.125
- w_down: bfloat16 [4864, 1792], P('head', 'seq'), may hold values from -0.078125 to 0.078125
Outputs:
- output: bfloat16 [2, 8192, 1792], P(None, 'seq', 'head')
- grad_input: bfloat16 [2, 8192, 1792], P(None, 'seq', 'head')
- grad_norm_gains: float32 [2, 1792], P(None, 'seq')
- grad_conv_filter: float32 [3, 1792], P(None, 'seq')
- grad_w_query: float32 [1792, 256], P('seq', 'head')
- grad_w_key: float32 [1792, 256], P('seq', 'head')
- grad_w_value: float32 [1792, 1792], P('seq', 'head')
- grad_w_wquery: float32 [1792, 1792], P('seq', 'head')
- grad_w_wkey: float32 [1792, 1792], P('seq', 'head')
- grad_w_conv_in: float32 [1792, 1792], P('seq', 'head')
- grad_w_conv_gate: float32 [1792, 1792], P('seq', 'head')
- grad_w_out: float32 [1792, 1792], P('head', 'seq')
- grad_w_gate: float32 [1792, 4864], P('seq', 'head')
- grad_w_up: float32 [1792, 4864], P('seq', 'head')
- grad_w_down: float32 [4864, 1792], P('head', 'seq')
The draws below stay inside these ranges and needn't reach their ends.
Inputs may be any that keep to these rules, and one draw needn't show every extreme that they name: `lengths`: in each row one document has exactly (61) * 128 tokens and each other document 1 to 128, so that the documents fill the 64 tiles. `doc_order`: each row is a permutation of 0 to 3.
All inputs are finite; a program needn't handle non-finite values.
Results may differ from the reference program's by a relative error of at most 0.018.
Values may be sent and summed in bfloat16 or wider, within the bound.
A program may use at most 640 MiB of HBM per device.

```python
import math
import jax
import jax.numpy as jnp
from jax import lax

D = 1792
HEADS = 16
FDIM = 16
FF = 4864
HDIM = 112
WIN = 64
KCONV = 3
TILE = 128
MB = 2
DOCS = 4
TOK_DEV = 512
TOKENS = 8192


def draw_lengths(key, part):
    key = jax.random.fold_in(key, 11)
    subkeys = jax.random.split(key, MB)

    def one_row(subkey):
        first_key, second_key = jax.random.split(subkey)
        long_doc = jax.random.randint(first_key, (), 0, DOCS)
        short_lengths = jax.random.randint(second_key, (DOCS,), 1, TILE + 1)
        longest = (TOKENS // TILE - DOCS + 1) * TILE
        return jnp.where(jnp.arange(DOCS) == long_doc, longest, short_lengths).astype(jnp.int32)
    return jax.vmap(one_row)(subkeys)


def draw_doc_order(key, part):
    key = jax.random.fold_in(key, 12)
    subkeys = jax.random.split(key, MB)

    def one_row(subkey):
        return jax.random.permutation(subkey, DOCS).astype(jnp.int32)
    return jax.vmap(one_row)(subkeys)


def steps_of(rng, extent, pieces, low, high):
    def one(position, blocks):
        heights = jax.random.uniform(jax.random.fold_in(jax.random.fold_in(rng, 6), position), (blocks,), jnp.float32, low / len(pieces), high / len(pieces))
        return jnp.repeat(jnp.exp(heights), extent[position] // blocks).reshape((-1,) + (1,) * (len(extent) - position - 1))

    factor_of = one(*pieces[0])
    for cut in pieces[1:]:
        factor_of = factor_of * one(*cut)
    return factor_of


def bell_draw(rng, dims, spread, reach, cuts=(), held_as=jnp.bfloat16):
    values = spread * jax.random.normal(rng, dims, jnp.float32)
    if cuts:
        values = values * steps_of(rng, dims, cuts, -0.22, 0.18)
    return jnp.clip(values, -reach, reach).astype(held_as)


def setup_inputs(seed: int = 0) -> dict:
    splits = jax.random.split(jax.random.key(seed), 18)
    layer_input = bell_draw(splits[0], (MB, TOKENS, D), 1.0, 6.0, ((1, 16), (2, 2)))
    cotangent = bell_draw(splits[1], (MB, TOKENS, D), 1.0, 6.0, ((1, 16), (2, 2)))
    lengths = draw_lengths(jax.random.fold_in(splits[17], 71), 0)
    doc_order = draw_doc_order(jax.random.fold_in(splits[17], 71), 0)
    norm_gains = jnp.clip(1.0 + 0.1 * jax.random.normal(splits[4], (2, D), jnp.float32), 0.5, 1.5).astype(jnp.bfloat16)
    conv_filter = bell_draw(splits[5], (KCONV, D), 0.6, 3.0, ((1, 16),))
    w_query = bell_draw(splits[6], (D, HEADS * FDIM), D ** -0.5, 0.125, ((0, 16), (1, 2)))
    w_key = bell_draw(splits[7], (D, HEADS * FDIM), D ** -0.5, 0.125, ((0, 16), (1, 2)))
    w_value = bell_draw(splits[8], (D, D), D ** -0.5, 0.125, ((0, 16), (1, 2)))
    w_wquery = bell_draw(splits[9], (D, D), D ** -0.5, 0.125, ((0, 16), (1, 2)))
    w_wkey = bell_draw(splits[10], (D, D), D ** -0.5, 0.125, ((0, 16), (1, 2)))
    w_conv_in = bell_draw(splits[11], (D, D), D ** -0.5, 0.125, ((0, 16), (1, 2)))
    w_conv_gate = bell_draw(splits[12], (D, D), D ** -0.5, 0.125, ((0, 16), (1, 2)))
    w_out = bell_draw(splits[13], (D, D), (D // 2) ** -0.5, 0.1875, ((0, 2), (1, 16)))
    w_gate = bell_draw(splits[14], (D, FF), D ** -0.5, 0.125, ((0, 16), (1, 2)))
    w_up = bell_draw(splits[15], (D, FF), D ** -0.5, 0.125, ((0, 16), (1, 2)))
    w_down = bell_draw(splits[16], (FF, D), FF ** -0.5, 0.078125, ((0, 2), (1, 16)))
    return dict(layer_input=layer_input, cotangent=cotangent, lengths=lengths, doc_order=doc_order, norm_gains=norm_gains, conv_filter=conv_filter, w_query=w_query, w_key=w_key, w_value=w_value, w_wquery=w_wquery, w_wkey=w_wkey, w_conv_in=w_conv_in, w_conv_gate=w_conv_gate, w_out=w_out, w_gate=w_gate, w_up=w_up, w_down=w_down)


@jax.custom_vjp
def low(v):
    return lax.optimization_barrier(v.astype(jnp.bfloat16)).astype(jnp.float32)

@jax.custom_vjp
def low_back(v):
    return v

def low_keep(v):
    return (low(v), None)

def low_pass(kept, grad):
    return (grad,)

def back_keep(v):
    return (v, None)

def back_low(kept, grad):
    return (low(grad),)
low.defvjp(low_keep, low_pass)
low_back.defvjp(back_keep, back_low)
highest = lax.Precision.HIGHEST

def matmul(left, right):
    return jnp.dot(left, right, precision=highest, preferred_element_type=jnp.float32)

def normalize(values):
    return values * lax.rsqrt(lax.optimization_barrier(jnp.mean(values * values, axis=-1, keepdims=True)) + 1e-05)

def feature_map(entries):
    halved = 0.5 * entries
    squares_map = halved[..., :, None] * halved[..., None, :]
    flattened = squares_map.reshape(entries.shape[:-1] + (entries.shape[-1] * entries.shape[-1],))
    unit_col = jnp.ones(entries.shape[:-1] + (1,), jnp.float32)
    return jnp.concatenate([unit_col, halved, flattened * (1.0 / math.sqrt(2.0))], axis=-1)

def layout(lengths, order, positions, tile_rows):
    count = lengths.shape[0]
    places = jnp.arange(count, dtype=jnp.int32)
    picked = (order[:, None] == places[None, :]).astype(jnp.int32)
    ordered = lax.optimization_barrier(jnp.sum(picked * lengths[None, :], axis=1, dtype=jnp.int32))
    tiles = (ordered + tile_rows - 1) // tile_rows
    first_tile = jnp.cumsum(tiles, dtype=jnp.int32) - tiles
    row_tile = positions // tile_rows
    doc_slot = lax.optimization_barrier(jnp.sum((row_tile[:, None] >= first_tile[None, :]).astype(jnp.int32), axis=1, dtype=jnp.int32)) - 1
    chosen = (doc_slot[:, None] == places[None, :]).astype(jnp.int32)
    doc_start = lax.optimization_barrier(jnp.sum(chosen * first_tile[None, :], axis=1, dtype=jnp.int32)) * tile_rows
    doc_length = lax.optimization_barrier(jnp.sum(chosen * ordered[None, :], axis=1, dtype=jnp.int32))
    is_valid = positions - doc_start < doc_length
    return (doc_slot, doc_start, is_valid)

def linear_out(queries, key_rows, values, state, total, doc_slot, doc_start, is_valid, block_start):
    row_count = queries.shape[0]
    head_count = queries.shape[1] // FDIM
    query_heads = queries.reshape(row_count, head_count, FDIM)
    key_heads = key_rows.reshape(row_count, head_count, FDIM)
    value_heads = values.reshape(row_count, head_count, -1)
    products = 0.25 * jnp.einsum('ihf,jhf->hij', query_heads, key_heads, precision=highest)
    kernel = 1.0 + products + 0.5 * products * products
    row_index = jnp.arange(row_count, dtype=jnp.int32)
    allowed = (row_index[None, :] <= row_index[:, None]) & (doc_slot[None, :] == doc_slot[:, None]) & (is_valid[None, :] | (row_index[None, :] == row_index[:, None]))
    weights = jnp.where(allowed[None], kernel, 0.0)
    numer = jnp.einsum('hij,jhd->ihd', low(weights), value_heads, precision=highest)
    denom = lax.optimization_barrier(jnp.sum(weights, axis=2)).T
    carried = (doc_start < block_start).astype(jnp.float32)
    mapped = low(feature_map(query_heads))
    numer = numer + carried[:, None, None] * jnp.einsum('ihp,hpd->ihd', mapped, state, precision=highest)
    denom = denom + carried[:, None] * jnp.einsum('ihp,hp->ih', mapped, total, precision=highest)
    return (numer / denom[:, :, None]).reshape(row_count, -1)

def linear_own(key_rows, values, doc_slot, doc_start, is_valid, block_start):
    row_count = key_rows.shape[0]
    head_count = key_rows.shape[1] // FDIM
    key_heads = key_rows.reshape(row_count, head_count, FDIM)
    value_heads = values.reshape(row_count, head_count, -1)
    last_doc = ((doc_slot == doc_slot[row_count - 1]) & is_valid).astype(jnp.float32)
    mapped = low(feature_map(key_heads)) * last_doc[:, None, None]
    state = jnp.einsum('jhp,jhd->hpd', mapped, value_heads, precision=highest)
    total = lax.optimization_barrier(jnp.sum(mapped, axis=0))
    return (state, total)

def window_out(queries, doc_slot, is_valid, positions, key_rows, values, key_slot, key_valid, key_place):
    row_count = queries.shape[0]
    head_count = queries.shape[1] // HDIM
    query_heads = queries.reshape(row_count, head_count, HDIM)
    key_heads = key_rows.reshape(-1, head_count, HDIM)
    value_heads = values.reshape(-1, head_count, HDIM)
    scores = jnp.einsum('ihd,jhd->hij', query_heads, key_heads, precision=highest) * (1.0 / math.sqrt(HDIM))
    distance = positions[:, None] - key_place[None, :]
    allowed = (distance >= 0) & (distance <= WIN) & (doc_slot[:, None] == key_slot[None, :]) & (key_valid[None, :] | (distance == 0))
    scores = jnp.where(allowed[None], scores, -1e+30)
    row_max = lax.optimization_barrier(jnp.max(scores, axis=2, keepdims=True))
    exponent = jnp.exp(scores - row_max)
    weights_soft = low(exponent / lax.optimization_barrier(jnp.sum(exponent, axis=2, keepdims=True)))
    return jnp.einsum('hij,jhd->ihd', weights_soft, value_heads, precision=highest).reshape(row_count, -1)

def conv_mix(normed_before, normed, taps, slot_before, doc_slot):
    row_count = normed.shape[0]
    stacked = jnp.concatenate([normed_before, normed], axis=0)
    slot_stack = jnp.concatenate([slot_before, doc_slot], axis=0)
    result = taps[0] * normed
    for shift_by in range(1, KCONV):
        first_row = KCONV - 1 - shift_by
        earlier = stacked[first_row:first_row + row_count]
        same_doc = (slot_stack[first_row:first_row + row_count] == doc_slot).astype(jnp.float32)[:, None]
        result = result + taps[shift_by] * earlier * same_doc
    return result

def linear_all(queries, key_rows, values, doc_slot, doc_start, is_valid):
    blocks = queries.shape[0] // TOK_DEV
    head_count = queries.shape[1] // FDIM
    phi_size = 1 + FDIM + FDIM * FDIM
    head_dim = values.shape[1] // head_count

    def split_rows(array):
        return array.reshape((blocks, TOK_DEV) + array.shape[1:])

    def advance(carry, item):
        state, total = carry
        block_query, block_key, block_value, block_slot, block_start_rows, block_valid, number = item
        block_start = number * TOK_DEV
        result = linear_out(block_query, block_key, block_value, state, total, block_slot, block_start_rows, block_valid, block_start)
        own_state, own_total = linear_own(block_key, block_value, block_slot, block_start_rows, block_valid, block_start)
        keep = 1.0 - (block_start_rows[TOK_DEV - 1] >= block_start).astype(jnp.float32)
        return ((keep * state + own_state, keep * total + own_total), result)
    initial = (jnp.zeros((head_count, phi_size, head_dim), jnp.float32), jnp.zeros((head_count, phi_size), jnp.float32))
    items = (split_rows(queries), split_rows(key_rows), split_rows(values), split_rows(doc_slot), split_rows(doc_start), split_rows(is_valid), jnp.arange(blocks, dtype=jnp.int32))
    _, stacked = lax.scan(jax.checkpoint(advance), initial, items)
    return stacked.reshape(queries.shape[0], -1)

def window_all(queries, key_rows, values, doc_slot, is_valid, positions):
    blocks = queries.shape[0] // TOK_DEV

    def widen(array, fill):
        return jnp.concatenate([jnp.full((WIN,) + array.shape[1:], fill, array.dtype), array], axis=0)
    keys_wide = widen(key_rows, 0.0)
    values_wide = widen(values, 0.0)
    slot_wide = widen(doc_slot, -1)
    valid_wide = widen(is_valid, False)
    place_wide = widen(positions, -1)

    def one_block(number):
        first_row = number * TOK_DEV

        def take_rows(array, size):
            return lax.dynamic_slice_in_dim(array, first_row, size, 0)
        return window_out(take_rows(queries, TOK_DEV), take_rows(doc_slot, TOK_DEV), take_rows(is_valid, TOK_DEV), take_rows(positions, TOK_DEV), take_rows(keys_wide, TOK_DEV + WIN), take_rows(values_wide, TOK_DEV + WIN), take_rows(slot_wide, TOK_DEV + WIN), take_rows(valid_wide, TOK_DEV + WIN), take_rows(place_wide, TOK_DEV + WIN))
    stacked = lax.map(jax.checkpoint(one_block), jnp.arange(blocks, dtype=jnp.int32))
    return stacked.reshape(queries.shape[0], -1)

def layer(params, input_rows, doc_slot, doc_start, is_valid, positions):
    gains, taps, w_query, w_key, w_value, w_wquery, w_wkey, w_conv_in, w_conv_gate, w_out, w_gate, w_up, w_down = params
    normed = low(normalize(input_rows) * gains[0])
    queries = low_back(low(matmul(normed, w_query)))
    key_rows = low_back(low(matmul(normed, w_key)))
    values = low_back(low(matmul(normed, w_value)))
    wqueries = low_back(low(matmul(normed, w_wquery)))
    wkeys = low_back(low(matmul(normed, w_wkey)))
    conv_gate = low_back(matmul(normed, w_conv_gate))
    before = jnp.zeros((KCONV - 1, normed.shape[1]), jnp.float32)
    slot_before = jnp.full((KCONV - 1,), -1, jnp.int32)
    conv = low(conv_mix(before, normed, taps, slot_before, doc_slot))
    conv_out = low_back(matmul(conv, w_conv_in)) * conv_gate
    linear = linear_all(queries, key_rows, values, doc_slot, doc_start, is_valid)
    window = window_all(wqueries, wkeys, values, doc_slot, is_valid, positions)
    mixed = low_back(low(linear + window + conv_out))
    resid = input_rows + matmul(mixed, w_out)
    second = low(normalize(resid) * gains[1])
    gate = low_back(matmul(second, w_gate))
    up_rows = low_back(matmul(second, w_up))
    hidden = low(jax.nn.silu(gate) * up_rows)
    return resid + matmul(hidden, w_down)

def reference(layer_input, cotangent, lengths, doc_order, norm_gains, conv_filter, w_query, w_key, w_value, w_wquery, w_wkey, w_conv_in, w_conv_gate, w_out, w_gate, w_up, w_down):
    params = tuple((piece.astype(jnp.float32) for piece in (norm_gains, conv_filter, w_query, w_key, w_value, w_wquery, w_wkey, w_conv_in, w_conv_gate, w_out, w_gate, w_up, w_down)))
    positions = jnp.arange(TOKENS, dtype=jnp.int32)
    outputs = []
    grads_in = []
    totals = [jnp.zeros_like(piece) for piece in params]
    for micro in range(MB):
        doc_slot, doc_start, is_valid = layout(lengths[micro], doc_order[micro], positions, TILE)

        def forward(weights_all, input_rows):
            return layer(weights_all, input_rows, doc_slot, doc_start, is_valid, positions)
        result, pull = jax.vjp(forward, params, layer_input[micro].astype(jnp.float32))
        grads_params, grad_rows = pull(cotangent[micro].astype(jnp.float32))
        outputs.append(result.astype(jnp.bfloat16))
        grads_in.append(grad_rows.astype(jnp.bfloat16))
        totals = [running + extra for running, extra in zip(totals, grads_params)]
    return (jnp.stack(outputs), jnp.stack(grads_in), totals[0], totals[1], totals[2], totals[3], totals[4], totals[5], totals[6], totals[7], totals[8], totals[9], totals[10], totals[11], totals[12])
```

```python
import functools
import math

import jax
import jax.numpy as jnp
import numpy as np
from jax import lax
from jax.experimental import pallas as pl
from jax.experimental.pallas import tpu as pltpu
from jax.sharding import PartitionSpec as P

FDIM = 16
HDIM = 112
WIN = 64
KCONV = 3
TILE = 128
LANES = 128
PHI = 160

f32 = jnp.float32
bf16 = jnp.bfloat16
VMEM_BYTES = 56 * 1024 * 1024


def mul(a, b):
    return lax.dot_general(a, b, (((1,), (0,)), ((), ())), preferred_element_type=f32)


def mul_t(a, b):
    return lax.dot_general(a, b, (((1,), (1,)), ((), ())), preferred_element_type=f32)


def t_mul(a, b):
    return lax.dot_general(a, b, (((0,), (0,)), ((), ())), preferred_element_type=f32)


def feature_tables(heads):
    left = np.zeros((heads, heads * FDIM, PHI), np.float32)
    right = np.zeros((heads, heads * FDIM, PHI), np.float32)
    consts = np.zeros((8, PHI), np.float32)
    at = 0
    for a in range(FDIM):
        for b in range(a, FDIM):
            for h in range(heads):
                left[h, h * FDIM + a, at] = 0.5
                right[h, h * FDIM + b, at] = 0.5
            consts[2, at] = 1.0 / math.sqrt(2.0)
            consts[3, at] = 1.0 if a == b else 2.0
            at += 1
    for a in range(FDIM):
        for h in range(heads):
            left[h, h * FDIM + a, at] = 0.5
        consts[1, at] = 1.0
        consts[2, at] = 1.0
        consts[3, at] = 1.0
        at += 1
    consts[0, at] = consts[1, at] = consts[2, at] = consts[3, at] = 1.0
    return jnp.asarray(left, bf16), jnp.asarray(right, bf16), jnp.asarray(consts)


def with_one(values):
    rows = values.shape[0]
    lane = lax.broadcasted_iota(jnp.int32, (rows, LANES - HDIM), 1)
    extra = jnp.where(lane == 0, 1.0, 0.0).astype(values.dtype)
    return jnp.concatenate([values, extra], axis=1)


def head_cols(h):
    return slice(h * HDIM, (h + 1) * HDIM)


def features(rows, left, right, consts):
    a = mul(rows, left) + consts[0:1]
    b = mul(rows, right) + consts[1:2]
    return a, b, (a * b * consts[2:3]).astype(bf16)


def own_kernel(ic, qk, v, left, right, consts, state):
    heads = v.shape[2] // HDIM
    width = qk.shape[2] // 2
    keys = qk[0, :, width:]
    last = ic[0, :, 2:3].astype(f32)
    table = consts[...]
    for h in range(heads):
        _, _, phi = features(keys, left[h], right[h], table)
        phi = (phi.astype(f32) * last).astype(bf16)
        state[0, h] = t_mul(phi, with_one(v[0, :, head_cols(h)])).astype(bf16)


def linear_mask(ic, ir, t):
    rows, cols = TILE, TILE * (t + 1)
    i = lax.broadcasted_iota(jnp.int32, (rows, cols), 0) + t * TILE
    j = lax.broadcasted_iota(jnp.int32, (rows, cols), 1)
    slot = ic[0, t * TILE : (t + 1) * TILE, 0:1]
    kslot = ir[0, 1:2, 0:cols]
    return ((kslot == slot) & (j <= i)) | (j == i)


def window_mask(ic, ir, t):
    rows, cols = TILE, TILE + WIN
    i = lax.broadcasted_iota(jnp.int32, (rows, cols), 0)
    j = lax.broadcasted_iota(jnp.int32, (rows, cols), 1) - WIN
    slot = ic[0, t * TILE : (t + 1) * TILE, 0:1]
    kslot = ir[0, 0:1, t * TILE : t * TILE + cols]
    return ((kslot == slot) & (j <= i) & (i - j <= WIN)) | (j == i)


def fill_masks(ic, ir, lmask, wmask, tiles):
    for t in range(tiles):
        lmask[t * TILE : (t + 1) * TILE, 0 : TILE * (t + 1)] = jnp.where(
            linear_mask(ic, ir, t), 1.0, 0.0
        )
        wmask[t * TILE : (t + 1) * TILE, :] = jnp.where(window_mask(ic, ir, t), 0.0, -1e30)


def window_probs(wq_rows, wk_rows, mask):
    scores = mul_t(wq_rows, wk_rows) * (1.0 / math.sqrt(HDIM)) + mask
    top = jnp.max(scores, axis=1, keepdims=True)
    exponent = jnp.exp(scores - top)
    return exponent / jnp.sum(exponent, axis=1, keepdims=True)


def head_rows(rows, h):
    lane = lax.broadcasted_iota(jnp.int32, rows.shape, 1)
    return jnp.where(lane // FDIM == h, rows.astype(f32), 0.0).astype(bf16)


def mix_kernel(
    ic, ir, qk, v, wq, wk, cg, ci, wkp, vp, prefix, left, right, consts,
    mixed, linear, rden, lmask, wmask, kext, vext,
):
    heads = v.shape[2] // HDIM
    rows = v.shape[1]
    tiles = rows // TILE
    width = qk.shape[2] // 2
    fill_masks(ic, ir, lmask, wmask, tiles)
    queries = qk[0, :, :width]
    keys = qk[0, :, width:]
    carried = ic[0, :, 1:2].astype(f32)
    table = consts[...]
    lane = lax.broadcasted_iota(jnp.int32, (rows, LANES), 1)
    inverse = jnp.zeros((rows, LANES), f32)
    kext[0:WIN, :] = wkp[0]
    kext[WIN:, :] = wk[0]
    vext[0:WIN, :] = vp[0]
    vext[WIN:, :] = v[0]
    for h in range(heads):
        hc = head_cols(h)
        vh = with_one(vext[:, hc])
        kh = kext[:, hc]
        qh = head_rows(queries, h)
        _, _, phi = features(queries, left[h], right[h], table)
        phi = (phi.astype(f32) * (carried * table[3:4])).astype(bf16)
        for t in range(tiles):
            r = slice(t * TILE, (t + 1) * TILE)
            n = TILE * (t + 1)
            a = 0.25 * mul_t(qh[r], keys[0:n])
            weight = ((1.0 + a + 0.5 * (a * a)) * lmask[r, 0:n]).astype(bf16)
            numer = mul(weight, vh[WIN : WIN + n]) + mul(phi[r], prefix[0, h])
            inv = 1.0 / numer[:, HDIM : HDIM + 1]
            inverse_t = jnp.where(lane[r] == h, inv, 0.0)
            lin = (numer * inv)[:, :HDIM]
            probs = window_probs(wq[0, r, hc], kh[r.start : r.start + TILE + WIN], wmask[r, :])
            win = mul(probs.astype(bf16), vh[r.start : r.start + TILE + WIN])[:, :HDIM]
            conv = ci[0, r, hc].astype(f32) * cg[0, r, hc].astype(f32)
            mixed[0, r, hc] = (lin + win + conv).astype(bf16)
            linear[0, r, hc] = lin.astype(bf16)
            if h == 0:
                rden[0, r, :] = inverse_t
            else:
                rden[0, r, :] += inverse_t


def d_numer(dm, linear, rden, h, r):
    hc = head_cols(h)
    inv = rden[0, r, h : h + 1]
    dn = dm[0, r, hc].astype(f32) * inv
    dd = -jnp.sum(dn * linear[0, r, hc].astype(f32), axis=1, keepdims=True)
    return dn, dd


def with_total(dn, dd):
    rows = dn.shape[0]
    high = dd.astype(bf16).astype(f32)
    lane = lax.broadcasted_iota(jnp.int32, (rows, LANES - HDIM), 1)
    extra = jnp.where(lane == 0, high, jnp.where(lane == 1, dd - high, 0.0))
    return jnp.concatenate([dn, extra], axis=1).astype(bf16)


def prefix_grad_kernel(ic, qk, dm, linear, rden, left, right, consts, d_prefix):
    heads = dm.shape[2] // HDIM
    rows = dm.shape[1]
    width = qk.shape[2] // 2
    queries = qk[0, :, :width]
    carried = ic[0, :, 1:2].astype(f32)
    table = consts[...]
    for h in range(heads):
        _, _, phi = features(queries, left[h], right[h], table)
        phi = (phi.astype(f32) * (carried * table[3:4])).astype(bf16)
        dn, dd = d_numer(dm, linear, rden, h, slice(0, rows))
        d_prefix[0, h] = t_mul(phi, with_total(dn, dd)).astype(bf16)


def mix_grad_kernel(
    ic, ir, qk, v, wq, wk, cg, ci, wkp, vp, prefix, left, right, consts, dm, linear, rden,
    dq, dk, dv, dwq, dwk, dcg, dci, dwkp, dvp, lmask, wmask, kext, vext, dqs, dks, dvs, dwks,
):
    heads = v.shape[2] // HDIM
    rows = v.shape[1]
    tiles = rows // TILE
    width = qk.shape[2] // 2
    fill_masks(ic, ir, lmask, wmask, tiles)
    queries = qk[0, :, :width]
    keys = qk[0, :, width:]
    carried = ic[0, :, 1:2].astype(f32)
    table = consts[...]
    kext[0:WIN, :] = wkp[0]
    kext[WIN:, :] = wk[0]
    vext[0:WIN, :] = vp[0]
    vext[WIN:, :] = v[0]
    grad_rows = dm[0].astype(f32)
    dci[0] = (grad_rows * cg[0].astype(f32)).astype(bf16)
    dcg[0] = (grad_rows * ci[0].astype(f32)).astype(bf16)
    lane_q = lax.broadcasted_iota(jnp.int32, (TILE, width), 1)
    lane_f = lax.broadcasted_iota(jnp.int32, (PHI, LANES), 1)
    dqs[...] = jnp.zeros_like(dqs)
    dks[...] = jnp.zeros_like(dks)
    for h in range(heads):
        hc = head_cols(h)
        vh = vext[:, hc]
        kh = kext[:, hc]
        qh = head_rows(queries, h)
        khead = head_rows(keys, h)
        state = prefix[0, h].astype(f32)
        state = jnp.where(lane_f == HDIM + 1, state[:, HDIM : HDIM + 1], state).astype(bf16)
        dvs[...] = jnp.zeros_like(dvs)
        dwks[...] = jnp.zeros_like(dwks)
        for t in range(tiles):
            r = slice(t * TILE, (t + 1) * TILE)
            n = TILE * (t + 1)
            e = slice(t * TILE, t * TILE + TILE + WIN)
            dmt = dm[0, r, hc]
            probs = window_probs(wq[0, r, hc], kh[e], wmask[r, :])
            dp = mul_t(dmt, vh[e])
            ds = probs * (dp - jnp.sum(dp * probs, axis=1, keepdims=True))
            ds = (ds * (1.0 / math.sqrt(HDIM))).astype(bf16)
            dwq[0, r, hc] = mul(ds, kh[e]).astype(bf16)
            dwks[e, :] += t_mul(ds, wq[0, r, hc])
            dvs[e, :] += t_mul(probs.astype(bf16), dmt)

            dn, dd = d_numer(dm, linear, rden, h, r)
            dnb = dn.astype(bf16)
            a = 0.25 * mul_t(qh[r], keys[0:n])
            mask = lmask[r, 0:n]
            weight = ((1.0 + a + 0.5 * (a * a)) * mask).astype(bf16)
            dkern = mul_t(dnb, vh[WIN : WIN + n]) + dd
            da = (dkern * (1.0 + a) * (0.25 * mask)).astype(bf16)
            dvs[WIN : WIN + n, :] += t_mul(weight, dnb)
            dks[0:n, :] += t_mul(da, qh[r])
            g = mul_t(with_total(dn, dd), state) * (
                carried[r] * (table[2:3] * table[3:4])
            )
            fa, fb, _ = features(queries[r], left[h], right[h], table)
            dqs[r, :] += (
                mul(da, khead[0:n])
                + mul_t((g * fb).astype(bf16), left[h])
                + mul_t((g * fa).astype(bf16), right[h])
            )
        dv[0, :, hc] = dvs[WIN:, :]
        dvp[0, :, hc] = dvs[0:WIN, :].astype(bf16)
        dwk[0, :, hc] = dwks[WIN:, :]
        dwkp[0, :, hc] = dwks[0:WIN, :].astype(bf16)
    dq[0] = dqs[...].astype(bf16)
    dk[0] = dks[...]


def finish_kernel(
    ic, qk, v, d_own, left, right, consts, dk, dv, dwk, dwq, dcg, dq, back_k, back_v, out
):
    heads = v.shape[2] // HDIM
    rows = v.shape[1]
    half = v.shape[2]
    width = qk.shape[2] // 2
    keys = qk[0, :, width:]
    last = ic[0, :, 2:3].astype(f32)
    table = consts[...]
    d_keys = dk[0]
    for h in range(heads):
        hc = head_cols(h)
        grad = d_own[0, h]
        fa, fb, phi = features(keys, left[h], right[h], table)
        phi = (phi.astype(f32) * last).astype(bf16)
        part = dv[0, :, hc] + mul(phi, grad)[:, :HDIM]
        out[0, 0 : rows - WIN, hc] = part[0 : rows - WIN].astype(bf16)
        out[0, rows - WIN :, hc] = (part[rows - WIN :] + back_v[0, :, hc].astype(f32)).astype(bf16)
        g = mul_t(with_one(v[0, :, hc]), grad) * (last * table[2:3])
        d_keys = (
            d_keys
            + mul_t((g * fb).astype(bf16), left[h])
            + mul_t((g * fa).astype(bf16), right[h])
        )
    out[0, :, half : 2 * half] = dwq[0]
    out[0, 0 : rows - WIN, 2 * half : 3 * half] = dwk[0, 0 : rows - WIN].astype(bf16)
    out[0, rows - WIN :, 2 * half : 3 * half] = (
        dwk[0, rows - WIN :] + back_k[0].astype(f32)
    ).astype(bf16)
    out[0, :, 3 * half : 4 * half] = dcg[0]
    out[0, :, 4 * half : 4 * half + width] = dq[0]
    out[0, :, 4 * half + width :] = d_keys.astype(bf16)


def micro_spec(array, block=None, at=0):
    shape = array.shape
    if block is None:
        return pl.BlockSpec((1,) + shape[1:], lambda m: (m,) + (0,) * (len(shape) - 1))
    return pl.BlockSpec((1, shape[1], block), lambda m: (m, 0, at))


def whole_spec(array):
    rank = len(array.shape)
    return pl.BlockSpec(array.shape, lambda m: (0,) * rank)


def call(kernel, micros, ins, outs, scratch, flops):
    return pl.pallas_call(
        kernel,
        grid=(micros,),
        in_specs=[spec for _, spec in ins],
        out_specs=[micro_spec(o) for o in outs],
        out_shape=[jax.ShapeDtypeStruct(o.shape, o.dtype) for o in outs],
        scratch_shapes=scratch,
        compiler_params=pltpu.CompilerParams(vmem_limit_bytes=VMEM_BYTES),
        cost_estimate=pl.CostEstimate(
            flops=flops,
            bytes_accessed=sum(math.prod(o.shape) * o.dtype.itemsize for o in outs) * 3,
            transcendentals=0,
        ),
    )(*[a for a, _ in ins])


def struct(*shape, dtype=bf16):
    return jax.ShapeDtypeStruct(shape, dtype)


def projected(proj, half):
    width = proj.shape[2] - 4 * half
    return [(proj, micro_spec(proj, half, i)) for i in range(4)] + [
        (proj, micro_spec(proj, width, 4 * half // width))
    ]


def own_states(ic, proj, half, tables):
    micros = proj.shape[0]
    heads = half // HDIM
    v, _, _, _, qk = projected(proj, half)
    ins = [(ic, micro_spec(ic)), qk, v] + [(t, whole_spec(t)) for t in tables]
    return call(own_kernel, micros, ins, [struct(micros, heads, PHI, LANES)], [], 10**9)[0]


def mix_forward(ic, ir, proj, half, conv_in, tail_k, tail_v, prefix, tables):
    micros, rows, _ = proj.shape
    v, wq, wk, cg, qk = projected(proj, half)
    rest = [(a, micro_spec(a)) for a in (conv_in, tail_k, tail_v, prefix)]
    ins = (
        [(ic, micro_spec(ic)), (ir, micro_spec(ir)), qk, v, wq, wk, cg]
        + rest
        + [(t, whole_spec(t)) for t in tables]
    )
    outs = [
        struct(micros, rows, half),
        struct(micros, rows, half),
        struct(micros, rows, LANES, dtype=f32),
    ]
    scratch = [
        pltpu.VMEM((rows, rows), f32),
        pltpu.VMEM((rows, TILE + WIN), f32),
        pltpu.VMEM((rows + WIN, half), bf16),
        pltpu.VMEM((rows + WIN, half), bf16),
    ]
    return call(mix_kernel, micros, ins, outs, scratch, 10**10)


def prefix_gradient(ic, proj, half, dm, linear, rden, tables):
    micros = proj.shape[0]
    heads = half // HDIM
    qk = projected(proj, half)[4]
    ins = (
        [(ic, micro_spec(ic)), qk]
        + [(a, micro_spec(a)) for a in (dm, linear, rden)]
        + [(t, whole_spec(t)) for t in tables]
    )
    return call(
        prefix_grad_kernel, micros, ins, [struct(micros, heads, PHI, LANES)], [], 10**9
    )[0]


def mix_backward(ic, ir, proj, half, conv_in, tail_k, tail_v, prefix, tables, dm, linear, rden):
    micros, rows, _ = proj.shape
    width = (proj.shape[2] - 4 * half) // 2
    v, wq, wk, cg, qk = projected(proj, half)
    ins = (
        [(ic, micro_spec(ic)), (ir, micro_spec(ir)), qk, v, wq, wk, cg]
        + [(a, micro_spec(a)) for a in (conv_in, tail_k, tail_v, prefix)]
        + [(t, whole_spec(t)) for t in tables]
        + [(a, micro_spec(a)) for a in (dm, linear, rden)]
    )
    outs = [
        struct(micros, rows, width),
        struct(micros, rows, width, dtype=f32),
        struct(micros, rows, half, dtype=f32),
        struct(micros, rows, half),
        struct(micros, rows, half, dtype=f32),
        struct(micros, rows, half),
        struct(micros, rows, half),
        struct(micros, WIN, half),
        struct(micros, WIN, half),
    ]
    scratch = [
        pltpu.VMEM((rows, rows), f32),
        pltpu.VMEM((rows, TILE + WIN), f32),
        pltpu.VMEM((rows + WIN, half), bf16),
        pltpu.VMEM((rows + WIN, half), bf16),
        pltpu.VMEM((rows, width), f32),
        pltpu.VMEM((rows, width), f32),
        pltpu.VMEM((rows + WIN, HDIM), f32),
        pltpu.VMEM((rows + WIN, HDIM), f32),
    ]
    return call(mix_grad_kernel, micros, ins, outs, scratch, 2 * 10**10)


def finish_gradients(ic, proj, half, d_own, tables, dk, dv, dwk, dwq, dcg, dq, back_k, back_v):
    micros = proj.shape[0]
    v, _, _, _, qk = projected(proj, half)
    ins = (
        [(ic, micro_spec(ic)), qk, v, (d_own, micro_spec(d_own))]
        + [(t, whole_spec(t)) for t in tables]
        + [(a, micro_spec(a)) for a in (dk, dv, dwk, dwq, dcg, dq, back_k, back_v)]
    )
    return call(finish_kernel, micros, ins, [struct(*proj.shape)], [], 2 * 10**9)[0]


def cut_axis(size):
    side = max(s for s in range(1, size + 1) if s**3 <= size and size % (s * s) == 0)
    return (size // (side * side), side, side)


def strides(dims):
    return (dims[1] * dims[2], dims[2], 1)


def coords(index, dims):
    return tuple((index // st) % d for st, d in zip(strides(dims), dims))


def ring_pairs(dims, axis, shift):
    stride, size = strides(dims)[axis], dims[axis]
    pairs = []
    for i in range(math.prod(dims)):
        c = (i // stride) % size
        pairs.append((i, i + ((c + shift) % size - c) * stride))
    return pairs


def along(x, dims, axis, shift):
    return lax.ppermute(x, "seq", ring_pairs(dims, axis, shift))


def gather_pieces(shard, order, dims):
    pieces = [(shard[None], [(0, 0, 0)])]
    for step, axis in enumerate(order):
        arrived = []
        for shift in range(1, dims[axis]):
            for piece, offsets in pieces:
                moved = [o[:axis] + (shift,) + o[axis + 1 :] for o in offsets]
                arrived.append((along(piece, dims, axis, -shift), moved))
        pieces = pieces + arrived
        if step == 0 and len(pieces) > 1:
            pieces = [
                (
                    jnp.concatenate([p for p, _ in pieces], axis=0),
                    [o for _, offsets in pieces for o in offsets],
                )
            ]
    return pieces


def lay_kernel(dims, rows, plan, *refs):
    ins, out, stage, taken, put = refs[: len(plan)], *refs[len(plan) :]
    here = coords(lax.axis_index("seq"), dims)
    loads, stores = [], []
    for ref, (column, offsets) in zip(ins, plan):
        for b, offset in enumerate(offsets):
            there = sum(
                lax.rem(c + o, d) * st for c, o, d, st in zip(here, offset, dims, strides(dims))
            )
            place = (pl.ds(pl.multiple_of(there * rows, rows), rows), pl.ds(column, ref.shape[2]))
            k = len(loads)
            loads.append(pltpu.make_async_copy(ref.at[b], stage.at[place], taken.at[k]))
            stores.append(pltpu.make_async_copy(stage.at[place], out.at[place], put.at[k]))
    for load in loads:
        load.start()
    for load, store in zip(loads, stores):
        load.wait()
        store.start()
    for store in stores:
        store.wait()


def lay_blocks(pieces, dims):
    blocks = jnp.concatenate([p for p, _ in pieces], axis=0)
    known = [coords_place(o, dims) for _, offsets in pieces for o in offsets]
    slot_of = jnp.asarray(np.argsort(np.array(known)), jnp.int32)
    here = coords(lax.axis_index("seq"), dims)
    there = coords(jnp.arange(math.prod(dims), dtype=jnp.int32), dims)
    offset = [lax.rem(t - h + d, d) for t, h, d in zip(there, here, dims)]
    return blocks[slot_of[coords_place(offset, dims)]].reshape(-1, blocks.shape[2])


def coords_place(offset, dims):
    return sum(o * st for o, st in zip(offset, strides(dims)))


def lay_out(parts, dims):
    plan, arrays, column = [], [], 0
    for pieces in parts:
        for piece, offsets in pieces:
            plan.append((column, offsets))
            arrays.append(piece)
        column += pieces[0][0].shape[2]
    rows = arrays[0].shape[1]
    if rows % (2 * 8):
        return jnp.concatenate([lay_blocks(pieces, dims) for pieces in parts], axis=1)
    count = sum(len(offsets) for _, offsets in plan)
    size = math.prod(dims) * rows * column * arrays[0].dtype.itemsize
    return pl.pallas_call(
        functools.partial(lay_kernel, dims, rows, plan),
        in_specs=[pl.BlockSpec(memory_space=pl.ANY)] * len(arrays),
        out_specs=pl.BlockSpec(memory_space=pl.ANY),
        out_shape=jax.ShapeDtypeStruct((math.prod(dims) * rows, column), arrays[0].dtype),
        scratch_shapes=[
            pltpu.VMEM((math.prod(dims) * rows, column), arrays[0].dtype),
            pltpu.SemaphoreType.DMA((count,)),
            pltpu.SemaphoreType.DMA((count,)),
        ],
        compiler_params=pltpu.CompilerParams(vmem_limit_bytes=VMEM_BYTES),
        cost_estimate=pl.CostEstimate(flops=0, bytes_accessed=2 * size, transcendentals=0),
    )(*arrays)


def gather_rows(shard, orders, dims):
    total, used, parts = sum(share for _, share in orders), 0, []
    columns, done = shard.shape[1], 0
    for order, share in orders:
        done += share
        end = columns if done == total else columns * done // total // LANES * LANES
        parts.append(gather_pieces(shard[:, used:end], order, dims))
        used = end
    return lay_out(parts, dims)


def scatter_part(grad, order, dims):
    rows = grad.shape[0] // math.prod(dims)
    here = coords(lax.axis_index("seq"), dims)
    x = grad.reshape(dims + (rows, grad.shape[1]))
    for axis in order:
        total = lax.dynamic_index_in_dim(x, here[axis], axis).astype(f32)
        for shift in range(1, dims[axis]):
            to = lax.rem(here[axis] + shift, dims[axis])
            total = total + along(
                lax.dynamic_index_in_dim(x, to, axis), dims, axis, shift
            ).astype(f32)
        x = total.astype(grad.dtype)
    return total.reshape(rows, grad.shape[1])


def scatter_rows(grad, orders, dims):
    total, used, parts = sum(share for _, share in orders), 0, []
    columns, done = grad.shape[1], 0
    for order, share in orders:
        done += share
        end = columns if done == total else columns * done // total // LANES * LANES
        parts.append(scatter_part(grad[:, used:end], order[::-1], dims))
        used = end
    return parts[0] if len(parts) == 1 else jnp.concatenate(parts, axis=1)


def other_core(x):
    return lax.ppermute(x, "head", [(0, 1), (1, 0)])


def both_halves(x):
    y = other_core(x)
    first = lax.axis_index("head") == 0
    return jnp.concatenate([jnp.where(first, x, y), jnp.where(first, y, x)], axis=-1)


def core_sum(x):
    low = x.astype(bf16)
    return low.astype(f32) + other_core(low).astype(f32)


def shifted(x, by):
    size = lax.axis_size("seq")
    return lax.ppermute(x, "seq", [(i, i + by) for i in range(size) if 0 <= i + by < size])


def layout(lengths, order, positions):
    places = jnp.arange(lengths.shape[0], dtype=jnp.int32)
    picked = (order[:, None] == places[None, :]).astype(jnp.int32)
    ordered = jnp.sum(picked * lengths[None, :], axis=1, dtype=jnp.int32)
    tiles = (ordered + TILE - 1) // TILE
    first_tile = jnp.cumsum(tiles, dtype=jnp.int32) - tiles
    row_tile = positions // TILE
    after = (row_tile[:, None] >= first_tile[None, :]).astype(jnp.int32)
    slot = jnp.sum(after, axis=1, dtype=jnp.int32) - 1
    chosen = (slot[:, None] == places[None, :]).astype(jnp.int32)
    start = jnp.sum(chosen * first_tile[None, :], axis=1, dtype=jnp.int32) * TILE
    length = jnp.sum(chosen * ordered[None, :], axis=1, dtype=jnp.int32)
    return slot, start, positions - start < length


def carry_over(own, starts, rows, dims, backward):
    me = lax.axis_index("seq")
    here = coords(me, dims)

    def unbroken(a, b):
        last = lax.dynamic_index_in_dim(starts, jnp.maximum(b, 0), 1, keepdims=False)
        return (a > b) | (last < a * rows)

    def weigh(flag, x):
        return jnp.where(flag[:, None, None, None], x.astype(f32), 0.0)

    result = None
    total = own
    for axis in (2, 1, 0):
        size, stride = dims[axis], strides(dims)[axis]
        base = me // (stride * size) * (stride * size)
        c = here[axis]
        if size == 1:
            continue

        def gap(j):
            if backward:
                return unbroken(base, base + j * stride - 1)
            return unbroken(base + (j + 1) * stride, base + size * stride - 1)

        added = weigh(gap(c), total)
        for shift in range(1, size):
            j = lax.rem(c + size - shift, size)
            got = along(total, dims, axis, shift)
            if backward:
                near = (j > c) & unbroken(me + 1, base + j * stride - 1)
            else:
                near = (j < c) & unbroken(base + (j + 1) * stride, me - 1)
            part = weigh(near, got)
            result = part if result is None else result + part
            added = added + weigh(gap(j), got)
        total = added.astype(own.dtype)
    return result.astype(own.dtype)


def rsq(v):
    return lax.rsqrt(jnp.mean(v * v, axis=-1, keepdims=True) + 1e-05)


def norm_back(v, r, gain, dy):
    inner = jnp.mean(v * gain * dy, axis=-1, keepdims=True)
    return r * gain * dy - v * (r * r * r * inner), jnp.sum(dy * v * r, axis=0)


def dot_nt(a, b):
    return mul_t(a, b)


def per_device(
    layer_input,
    cotangent,
    lengths,
    doc_order,
    norm_gains,
    conv_filter,
    w_query,
    w_key,
    w_value,
    w_wquery,
    w_wkey,
    w_conv_in,
    w_conv_gate,
    w_out,
    w_gate,
    w_up,
    w_down,
):
    micros, rows, half = layer_input.shape
    dims = cut_axis(lax.axis_size("seq"))
    me = lax.axis_index("seq")
    head = lax.axis_index("head")
    place = me * rows
    tables = feature_tables(half // HDIM)
    qk = w_query.shape[1]
    ff = w_gate.shape[1]
    zyx, zxy, xzy, yzx = (0, 1, 2), (0, 2, 1), (2, 0, 1), (1, 0, 2)

    small = jnp.concatenate([norm_gains, conv_filter], axis=0).T
    small = jnp.pad(small, ((0, 0), (0, LANES - small.shape[1])))
    pack_in = jnp.concatenate([w_value, w_wquery, w_wkey, w_conv_gate, w_query, w_key], axis=1)
    pack_ff = jnp.concatenate([w_gate, w_up], axis=1)
    wide = [(zyx, 1), (zxy, 1)]
    narrow = [(xzy, 10), (yzx, 9)]
    small_all = gather_rows(small, [(zyx, 1)], dims)
    full_in = gather_rows(pack_in, wide, dims)
    full_conv = gather_rows(w_conv_in, [(xzy, 1)], dims)
    full_out = gather_rows(w_out.T, [(yzx, 1)], dims)
    full_ff = gather_rows(pack_ff, wide, dims)
    full_down = gather_rows(w_down.T, narrow, dims)
    vectors = small_all[:, : norm_gains.shape[0] + KCONV].astype(f32).T
    gain1, gain2 = vectors[0:1], vectors[1:2]
    taps = vectors[2:]

    positions = place + jnp.arange(rows, dtype=jnp.int32)
    window_place = place - WIN + jnp.arange(WIN, dtype=jnp.int32)
    conv_place = place - (KCONV - 1) + jnp.arange(KCONV - 1, dtype=jnp.int32)
    ends = (jnp.arange(lax.axis_size("seq"), dtype=jnp.int32) + 1) * rows - 1
    info_cols, info_rows, starts, same = [], [], [], []
    for m in range(micros):
        slot, start, valid = layout(lengths[m], doc_order[m], positions)
        wslot, _, wvalid = layout(lengths[m], doc_order[m], window_place)
        cslot, _, _ = layout(lengths[m], doc_order[m], conv_place)
        starts.append(layout(lengths[m], doc_order[m], ends)[1])
        last = (slot == slot[rows - 1]) & valid
        cols = jnp.stack([slot, (start < place).astype(jnp.int32), last.astype(jnp.int32)], axis=1)
        info_cols.append(jnp.pad(cols, ((0, 0), (0, 5))))
        own = jnp.where(valid, slot, -1)
        ext = jnp.concatenate([jnp.where(wvalid, wslot, -1), own])
        ext = jnp.pad(ext, (0, WIN), constant_values=-1)
        own = jnp.pad(own, (0, 2 * WIN), constant_values=-1)
        info_rows.append(jnp.pad(jnp.stack([ext, own]), ((0, 6), (0, 0))))
        stack = jnp.concatenate([cslot, slot])
        same.append(
            jnp.stack(
                [
                    stack[KCONV - 1 - s : KCONV - 1 - s + rows] == slot
                    for s in range(1, KCONV)
                ]
            )
        )
    ic, ir, starts = jnp.stack(info_cols), jnp.stack(info_rows), jnp.stack(starts)
    same = jnp.stack(same).astype(f32)[..., None]

    x_low = both_halves(layer_input)
    cot_low = both_halves(cotangent)
    x = x_low.astype(f32)
    r1 = rsq(x)
    h1 = (x * r1 * gain1).astype(bf16)
    width = h1.shape[2]
    h1_prev = shifted(h1[:, rows - (KCONV - 1) :], 1)
    flat_h1 = h1.reshape(micros * rows, width)
    proj = mul(flat_h1, full_in).astype(bf16).reshape(micros, rows, -1)

    tail_v = shifted(proj[:, rows - WIN :, :half], 1)
    tail_k = shifted(proj[:, rows - WIN :, 2 * half : 3 * half], 1)
    own = own_states(ic, proj, half, tables)
    prefix = carry_over(own, starts, rows, dims, False)

    stacked = jnp.concatenate([h1_prev, h1], axis=1)
    h1f = h1.astype(f32)
    earlier = [
        stacked[:, KCONV - 1 - s : KCONV - 1 - s + rows].astype(f32) * same[:, s - 1]
        for s in range(1, KCONV)
    ]
    conv = taps[0] * h1f
    for s in range(1, KCONV):
        conv = conv + taps[s] * earlier[s - 1]
    conv = conv.astype(bf16)
    flat_conv = conv.reshape(micros * rows, width)
    conv_in = mul(flat_conv, full_conv).astype(bf16).reshape(micros, rows, half)

    mixed, linear, rden = mix_forward(
        ic, ir, proj, half, conv_in, tail_k, tail_v, prefix, tables
    )
    flat_mixed = mixed.reshape(micros * rows, half)
    resid = x.reshape(micros * rows, width) + core_sum(mul_t(flat_mixed, full_out))

    r2 = rsq(resid)
    h2 = (resid * r2 * gain2).astype(bf16)
    gate_up = mul(h2, full_ff).astype(bf16)
    gate, up = gate_up[:, :ff].astype(f32), gate_up[:, ff:].astype(f32)
    sig = 1.0 / (1.0 + jnp.exp(-gate))
    hidden = (gate * sig * up).astype(bf16)
    flat_cot = cot_low.reshape(micros * rows, width)
    grad_down = t_mul(flat_cot, hidden).astype(bf16)
    sum_down = scatter_rows(grad_down, narrow, dims)
    ffn = mul_t(hidden, full_down).astype(bf16)

    def pick(a, which):
        return lax.dynamic_slice_in_dim(a, which * half, half, a.ndim - 1)

    ffn_other = other_core(pick(ffn, 1 - head))
    output = pick(resid, head) + (pick(ffn, head).astype(f32) + ffn_other.astype(f32))
    output = output.astype(bf16).reshape(micros, rows, half)

    d_hidden = mul(flat_cot, full_down)
    d_gate = (d_hidden * up * (sig * (1.0 + gate * (1.0 - sig)))).astype(bf16)
    d_up = (d_hidden * (gate * sig)).astype(bf16)
    d_ff = jnp.concatenate([d_gate, d_up], axis=1)
    grad_ff = t_mul(h2, d_ff).astype(bf16)
    sum_ff = scatter_rows(grad_ff, wide, dims)
    d_h2 = core_sum(mul_t(d_ff, full_ff))
    d_resid, d_gain2 = norm_back(resid, r2, gain2, d_h2)
    d_resid = flat_cot.astype(f32) + d_resid
    d_resid_low = d_resid.astype(bf16)

    grad_out = t_mul(d_resid_low, flat_mixed).astype(bf16)
    sum_out = scatter_rows(grad_out, [(yzx, 1)], dims)
    d_mixed = mul(d_resid_low, full_out).astype(bf16).reshape(micros, rows, half)
    d_prefix = prefix_gradient(ic, proj, half, d_mixed, linear, rden, tables)
    d_own = carry_over(d_prefix, starts, rows, dims, True)
    dq, dk, dv, dwq, dwk, dcg, dci, back_k, back_v = mix_backward(
        ic, ir, proj, half, conv_in, tail_k, tail_v, prefix, tables, d_mixed, linear, rden
    )
    back_k = shifted(back_k, -1)
    back_v = shifted(back_v, -1)
    flat_dci = dci.reshape(micros * rows, half)
    grad_conv = t_mul(flat_conv, flat_dci).astype(bf16)
    sum_conv = scatter_rows(grad_conv, [(xzy, 1)], dims)
    d_conv = mul_t(flat_dci, full_conv).reshape(micros, rows, width)
    d_h1 = taps[0] * d_conv
    d_taps = [jnp.sum(d_conv * h1f, axis=(0, 1))]
    before = jnp.zeros((micros, KCONV - 1, width), f32)
    for s in range(1, KCONV):
        through = d_conv * same[:, s - 1]
        d_taps.append(jnp.sum(d_conv * earlier[s - 1], axis=(0, 1)))
        moved = taps[s] * through
        d_h1 = d_h1 + jnp.pad(moved[:, s:], ((0, 0), (0, s), (0, 0)))
        before = before + jnp.pad(moved[:, :s], ((0, 0), (KCONV - 1 - s, 0), (0, 0)))
    returned = shifted(before.astype(bf16), -1).astype(f32)
    d_h1 = d_h1 + jnp.pad(returned, ((0, 0), (rows - (KCONV - 1), 0), (0, 0)))
    d_proj = finish_gradients(
        ic, proj, half, d_own, tables, dk, dv, dwk, dwq, dcg, dq, back_k, back_v
    ).reshape(micros * rows, -1)
    grad_in = t_mul(flat_h1, d_proj).astype(bf16)
    sum_in = scatter_rows(grad_in, wide, dims)
    d_h1 = core_sum(d_h1.reshape(micros * rows, width) + mul_t(d_proj, full_in))
    d_x, d_gain1 = norm_back(
        x.reshape(micros * rows, width), r1.reshape(micros * rows, 1), gain1, d_h1
    )
    grad_input = pick(d_resid + d_x, head).astype(bf16).reshape(micros, rows, half)

    d_taps = jnp.stack(d_taps)
    d_taps = d_taps + other_core(d_taps)
    d_small = jnp.concatenate([d_gain1[None], d_gain2[None], d_taps], axis=0).T
    d_small = jnp.pad(d_small, ((0, 0), (0, LANES - d_small.shape[1])))
    sum_small = scatter_rows(d_small, [(zyx, 1)], dims).T
    gains_count = norm_gains.shape[0]
    return (
        output,
        grad_input,
        sum_small[:gains_count],
        sum_small[gains_count : gains_count + KCONV],
        sum_in[:, 4 * half : 4 * half + qk],
        sum_in[:, 4 * half + qk :],
        sum_in[:, :half],
        sum_in[:, half : 2 * half],
        sum_in[:, 2 * half : 3 * half],
        sum_conv,
        sum_in[:, 3 * half : 4 * half],
        sum_out.T,
        sum_ff[:, :ff],
        sum_ff[:, ff:],
        sum_down.T,
    )


def solution(mesh):
    rows_split = P(None, "seq", "head")
    vectors = P(None, "seq")
    by_rows = P("seq", "head")
    by_columns = P("head", "seq")
    weights = (by_rows,) * 7 + (by_columns, by_rows, by_rows, by_columns)
    return jax.shard_map(
        per_device,
        mesh=mesh,
        in_specs=(rows_split, rows_split, P(), P(), vectors, vectors) + weights,
        out_specs=(rows_split, rows_split, vectors, vectors) + weights,
        check_vma=False,
    )
```

```python
import functools
import math

import jax
import jax.numpy as jnp
import numpy as np
from jax import lax
from jax.experimental import pallas as pl
from jax.experimental.pallas import tpu as pltpu
from jax.sharding import PartitionSpec as P

FDIM = 16
HDIM = 112
WIN = 64
KCONV = 3
TILE = 128
LANES = 128
PHI = 160

f32 = jnp.float32
bf16 = jnp.bfloat16
VMEM_BYTES = 60 * 1024 * 1024
MESH = pl.DeviceIdType.MESH

ZYX, ZXY, XZY, YZX, XYZ, YXZ = (0, 1, 2), (0, 2, 1), (2, 0, 1), (1, 0, 2), (2, 1, 0), (1, 2, 0)
FIRST = [(ZXY, 4), (ZXY, 5), (ZYX, 3), (ZXY, 4), (YZX, 3), (ZYX, 3), (ZXY, 5), (ZYX, 5), (YXZ, 4), (XZY, 5), (ZYX, 4)]
LAST = [(XZY, 5), (ZXY, 5), (YXZ, 3), (ZYX, 7), (YZX, 3), (ZYX, 3), (ZXY, 4), (ZYX, 3)]


def mul(a, b):
    return lax.dot_general(a, b, (((1,), (0,)), ((), ())), preferred_element_type=f32)


def mul_t(a, b):
    return lax.dot_general(a, b, (((1,), (1,)), ((), ())), preferred_element_type=f32)


def t_mul(a, b):
    return lax.dot_general(a, b, (((0,), (0,)), ((), ())), preferred_element_type=f32)


def feature_tables(heads):
    left = np.zeros((heads, heads * FDIM, PHI), np.float32)
    right = np.zeros((heads, heads * FDIM, PHI), np.float32)
    consts = np.zeros((8, PHI), np.float32)
    at = 0
    for a in range(FDIM):
        for b in range(a, FDIM):
            for h in range(heads):
                left[h, h * FDIM + a, at] = 0.5
                right[h, h * FDIM + b, at] = 0.5
            consts[2, at] = 1.0 / math.sqrt(2.0)
            consts[3, at] = 1.0 if a == b else 2.0
            at += 1
    for a in range(FDIM):
        for h in range(heads):
            left[h, h * FDIM + a, at] = 0.5
        consts[1, at] = 1.0
        consts[2, at] = 1.0
        consts[3, at] = 1.0
        at += 1
    consts[0, at] = consts[1, at] = consts[2, at] = consts[3, at] = 1.0
    return jnp.asarray(left, bf16), jnp.asarray(right, bf16), jnp.asarray(consts)


def with_one(values):
    rows = values.shape[0]
    lane = lax.broadcasted_iota(jnp.int32, (rows, LANES - HDIM), 1)
    extra = jnp.where(lane == 0, 1.0, 0.0).astype(values.dtype)
    return jnp.concatenate([values, extra], axis=1)


def head_cols(h):
    return slice(h * HDIM, (h + 1) * HDIM)


def features(rows, left, right, consts):
    a = mul(rows, left) + consts[0:1]
    b = mul(rows, right) + consts[1:2]
    return a, b, (a * b * consts[2:3]).astype(bf16)


def own_kernel(ic, qk, v, left, right, consts, state):
    heads = v.shape[2] // HDIM
    width = qk.shape[2] // 2
    keys = qk[0, :, width:]
    last = ic[0, :, 2:3].astype(f32)
    table = consts[...]
    for h in range(heads):
        _, _, phi = features(keys, left[h], right[h], table)
        phi = (phi.astype(f32) * last).astype(bf16)
        state[0, h] = t_mul(phi, with_one(v[0, :, head_cols(h)])).astype(bf16)


def linear_mask(ic, ir, t):
    rows, cols = TILE, TILE * (t + 1)
    i = lax.broadcasted_iota(jnp.int32, (rows, cols), 0) + t * TILE
    j = lax.broadcasted_iota(jnp.int32, (rows, cols), 1)
    slot = ic[0, t * TILE : (t + 1) * TILE, 0:1]
    kslot = ir[0, 1:2, 0:cols]
    return ((kslot == slot) & (j <= i)) | (j == i)


def window_mask(ic, ir, t):
    rows, cols = TILE, TILE + WIN
    i = lax.broadcasted_iota(jnp.int32, (rows, cols), 0)
    j = lax.broadcasted_iota(jnp.int32, (rows, cols), 1) - WIN
    slot = ic[0, t * TILE : (t + 1) * TILE, 0:1]
    kslot = ir[0, 0:1, t * TILE : t * TILE + cols]
    return ((kslot == slot) & (j <= i) & (i - j <= WIN)) | (j == i)


def fill_masks(ic, ir, lmask, wmask, tiles):
    for t in range(tiles):
        lmask[t * TILE : (t + 1) * TILE, 0 : TILE * (t + 1)] = jnp.where(
            linear_mask(ic, ir, t), 1.0, 0.0
        )
        wmask[t * TILE : (t + 1) * TILE, :] = jnp.where(window_mask(ic, ir, t), 0.0, -1e30)


def window_probs(wq_rows, wk_rows, mask):
    scores = mul_t(wq_rows, wk_rows) * (1.0 / math.sqrt(HDIM)) + mask
    top = jnp.max(scores, axis=1, keepdims=True)
    exponent = jnp.exp(scores - top)
    return exponent / jnp.sum(exponent, axis=1, keepdims=True)


def head_rows(rows, h):
    lane = lax.broadcasted_iota(jnp.int32, rows.shape, 1)
    return jnp.where(lane // FDIM == h, rows.astype(f32), 0.0).astype(bf16)


def mix_kernel(
    ic, ir, qk, v, wq, wk, cg, ci, wkp, vp, prefix, left, right, consts,
    mixed, linear, rden, lmask, wmask, kext, vext,
):
    heads = v.shape[2] // HDIM
    rows = v.shape[1]
    tiles = rows // TILE
    width = qk.shape[2] // 2
    fill_masks(ic, ir, lmask, wmask, tiles)
    queries = qk[0, :, :width]
    keys = qk[0, :, width:]
    carried = ic[0, :, 1:2].astype(f32)
    table = consts[...]
    lane = lax.broadcasted_iota(jnp.int32, (rows, LANES), 1)
    inverse = jnp.zeros((rows, LANES), f32)
    kext[0:WIN, :] = wkp[0]
    kext[WIN:, :] = wk[0]
    vext[0:WIN, :] = vp[0]
    vext[WIN:, :] = v[0]
    for h in range(heads):
        hc = head_cols(h)
        vh = with_one(vext[:, hc])
        kh = kext[:, hc]
        qh = head_rows(queries, h)
        _, _, phi = features(queries, left[h], right[h], table)
        phi = (phi.astype(f32) * (carried * table[3:4])).astype(bf16)
        for t in range(tiles):
            r = slice(t * TILE, (t + 1) * TILE)
            n = TILE * (t + 1)
            a = 0.25 * mul_t(qh[r], keys[0:n])
            weight = ((1.0 + a + 0.5 * (a * a)) * lmask[r, 0:n]).astype(bf16)
            numer = mul(weight, vh[WIN : WIN + n]) + mul(phi[r], prefix[0, h])
            inv = 1.0 / numer[:, HDIM : HDIM + 1]
            inverse_t = jnp.where(lane[r] == h, inv, 0.0)
            lin = (numer * inv)[:, :HDIM]
            probs = window_probs(wq[0, r, hc], kh[r.start : r.start + TILE + WIN], wmask[r, :])
            win = mul(probs.astype(bf16), vh[r.start : r.start + TILE + WIN])[:, :HDIM]
            conv = ci[0, r, hc].astype(f32) * cg[0, r, hc].astype(f32)
            mixed[0, r, hc] = (lin + win + conv).astype(bf16)
            linear[0, r, hc] = lin.astype(bf16)
            if h == 0:
                rden[0, r, :] = inverse_t
            else:
                rden[0, r, :] += inverse_t


def d_numer(dm, linear, rden, h, r):
    hc = head_cols(h)
    inv = rden[0, r, h : h + 1]
    dn = dm[0, r, hc].astype(f32) * inv
    dd = -jnp.sum(dn * linear[0, r, hc].astype(f32), axis=1, keepdims=True)
    return dn, dd


def with_total(dn, dd):
    rows = dn.shape[0]
    high = dd.astype(bf16).astype(f32)
    lane = lax.broadcasted_iota(jnp.int32, (rows, LANES - HDIM), 1)
    extra = jnp.where(lane == 0, high, jnp.where(lane == 1, dd - high, 0.0))
    return jnp.concatenate([dn, extra], axis=1).astype(bf16)


def prefix_grad_kernel(ic, qk, dm, linear, rden, left, right, consts, d_prefix):
    heads = dm.shape[2] // HDIM
    rows = dm.shape[1]
    width = qk.shape[2] // 2
    queries = qk[0, :, :width]
    carried = ic[0, :, 1:2].astype(f32)
    table = consts[...]
    for h in range(heads):
        _, _, phi = features(queries, left[h], right[h], table)
        phi = (phi.astype(f32) * (carried * table[3:4])).astype(bf16)
        dn, dd = d_numer(dm, linear, rden, h, slice(0, rows))
        d_prefix[0, h] = t_mul(phi, with_total(dn, dd)).astype(bf16)


def mix_grad_kernel(
    ic, ir, qk, v, wq, wk, cg, ci, wkp, vp, prefix, left, right, consts, dm, linear, rden,
    dq, dk, dv, dwq, dwk, dcg, dci, dwkp, dvp, lmask, wmask, kext, vext, dqs, dks, dvs, dwks,
):
    heads = v.shape[2] // HDIM
    rows = v.shape[1]
    tiles = rows // TILE
    width = qk.shape[2] // 2
    fill_masks(ic, ir, lmask, wmask, tiles)
    queries = qk[0, :, :width]
    keys = qk[0, :, width:]
    carried = ic[0, :, 1:2].astype(f32)
    table = consts[...]
    kext[0:WIN, :] = wkp[0]
    kext[WIN:, :] = wk[0]
    vext[0:WIN, :] = vp[0]
    vext[WIN:, :] = v[0]
    grad_rows = dm[0].astype(f32)
    dci[0] = (grad_rows * cg[0].astype(f32)).astype(bf16)
    dcg[0] = (grad_rows * ci[0].astype(f32)).astype(bf16)
    lane_q = lax.broadcasted_iota(jnp.int32, (TILE, width), 1)
    lane_f = lax.broadcasted_iota(jnp.int32, (PHI, LANES), 1)
    dqs[...] = jnp.zeros_like(dqs)
    dks[...] = jnp.zeros_like(dks)
    for h in range(heads):
        hc = head_cols(h)
        vh = vext[:, hc]
        kh = kext[:, hc]
        qh = head_rows(queries, h)
        khead = head_rows(keys, h)
        state = prefix[0, h].astype(f32)
        state = jnp.where(lane_f == HDIM + 1, state[:, HDIM : HDIM + 1], state).astype(bf16)
        dvs[...] = jnp.zeros_like(dvs)
        dwks[...] = jnp.zeros_like(dwks)
        for t in range(tiles):
            r = slice(t * TILE, (t + 1) * TILE)
            n = TILE * (t + 1)
            e = slice(t * TILE, t * TILE + TILE + WIN)
            dmt = dm[0, r, hc]
            probs = window_probs(wq[0, r, hc], kh[e], wmask[r, :])
            dp = mul_t(dmt, vh[e])
            ds = probs * (dp - jnp.sum(dp * probs, axis=1, keepdims=True))
            ds = (ds * (1.0 / math.sqrt(HDIM))).astype(bf16)
            dwq[0, r, hc] = mul(ds, kh[e]).astype(bf16)
            dwks[e, :] += t_mul(ds, wq[0, r, hc])
            dvs[e, :] += t_mul(probs.astype(bf16), dmt)

            dn, dd = d_numer(dm, linear, rden, h, r)
            dnb = dn.astype(bf16)
            a = 0.25 * mul_t(qh[r], keys[0:n])
            mask = lmask[r, 0:n]
            weight = ((1.0 + a + 0.5 * (a * a)) * mask).astype(bf16)
            dkern = mul_t(dnb, vh[WIN : WIN + n]) + dd
            da = (dkern * (1.0 + a) * (0.25 * mask)).astype(bf16)
            dvs[WIN : WIN + n, :] += t_mul(weight, dnb)
            dks[0:n, :] += t_mul(da, qh[r])
            g = mul_t(with_total(dn, dd), state) * (
                carried[r] * (table[2:3] * table[3:4])
            )
            fa, fb, _ = features(queries[r], left[h], right[h], table)
            dqs[r, :] += (
                mul(da, khead[0:n])
                + mul_t((g * fb).astype(bf16), left[h])
                + mul_t((g * fa).astype(bf16), right[h])
            )
        dv[0, :, hc] = dvs[WIN:, :]
        dvp[0, :, hc] = dvs[0:WIN, :].astype(bf16)
        dwk[0, :, hc] = dwks[WIN:, :]
        dwkp[0, :, hc] = dwks[0:WIN, :].astype(bf16)
    dq[0] = dqs[...].astype(bf16)
    dk[0] = dks[...]


def finish_kernel(
    ic, qk, v, d_own, left, right, consts, dk, dv, dwk, dwq, dcg, dq, back_k, back_v, out
):
    heads = v.shape[2] // HDIM
    rows = v.shape[1]
    half = v.shape[2]
    width = qk.shape[2] // 2
    keys = qk[0, :, width:]
    last = ic[0, :, 2:3].astype(f32)
    table = consts[...]
    d_keys = dk[0]
    for h in range(heads):
        hc = head_cols(h)
        grad = d_own[0, h]
        fa, fb, phi = features(keys, left[h], right[h], table)
        phi = (phi.astype(f32) * last).astype(bf16)
        part = dv[0, :, hc] + mul(phi, grad)[:, :HDIM]
        out[0, 0 : rows - WIN, hc] = part[0 : rows - WIN].astype(bf16)
        out[0, rows - WIN :, hc] = (part[rows - WIN :] + back_v[0, :, hc].astype(f32)).astype(bf16)
        g = mul_t(with_one(v[0, :, hc]), grad) * (last * table[2:3])
        d_keys = (
            d_keys
            + mul_t((g * fb).astype(bf16), left[h])
            + mul_t((g * fa).astype(bf16), right[h])
        )
    out[0, :, half : 2 * half] = dwq[0]
    out[0, 0 : rows - WIN, 2 * half : 3 * half] = dwk[0, 0 : rows - WIN].astype(bf16)
    out[0, rows - WIN :, 2 * half : 3 * half] = (
        dwk[0, rows - WIN :] + back_k[0].astype(f32)
    ).astype(bf16)
    out[0, :, 3 * half : 4 * half] = dcg[0]
    out[0, :, 4 * half : 4 * half + width] = dq[0]
    out[0, :, 4 * half + width :] = d_keys.astype(bf16)


def micro_spec(array, block=None, at=0):
    shape = array.shape
    if block is None:
        return pl.BlockSpec((1,) + shape[1:], lambda m: (m,) + (0,) * (len(shape) - 1))
    return pl.BlockSpec((1, shape[1], block), lambda m: (m, 0, at))


def whole_spec(array):
    rank = len(array.shape)
    return pl.BlockSpec(array.shape, lambda m: (0,) * rank)


def call(kernel, micros, ins, outs, scratch, flops):
    return pl.pallas_call(
        kernel,
        grid=(micros,),
        in_specs=[spec for _, spec in ins],
        out_specs=[micro_spec(o) for o in outs],
        out_shape=[jax.ShapeDtypeStruct(o.shape, o.dtype) for o in outs],
        scratch_shapes=scratch,
        compiler_params=pltpu.CompilerParams(vmem_limit_bytes=VMEM_BYTES),
        cost_estimate=pl.CostEstimate(
            flops=flops,
            bytes_accessed=sum(math.prod(o.shape) * o.dtype.itemsize for o in outs) * 3,
            transcendentals=0,
        ),
    )(*[a for a, _ in ins])


def struct(*shape, dtype=bf16):
    return jax.ShapeDtypeStruct(shape, dtype)


def projected(proj, half):
    width = proj.shape[2] - 4 * half
    return [(proj, micro_spec(proj, half, i)) for i in range(4)] + [
        (proj, micro_spec(proj, width, 4 * half // width))
    ]


def own_states(ic, proj, half, tables):
    micros = proj.shape[0]
    heads = half // HDIM
    v, _, _, _, qk = projected(proj, half)
    ins = [(ic, micro_spec(ic)), qk, v] + [(t, whole_spec(t)) for t in tables]
    return call(own_kernel, micros, ins, [struct(micros, heads, PHI, LANES)], [], 10**9)[0]


def mix_forward(ic, ir, proj, half, conv_in, tail_k, tail_v, prefix, tables):
    micros, rows, _ = proj.shape
    v, wq, wk, cg, qk = projected(proj, half)
    rest = [(a, micro_spec(a)) for a in (conv_in, tail_k, tail_v, prefix)]
    ins = (
        [(ic, micro_spec(ic)), (ir, micro_spec(ir)), qk, v, wq, wk, cg]
        + rest
        + [(t, whole_spec(t)) for t in tables]
    )
    outs = [
        struct(micros, rows, half),
        struct(micros, rows, half),
        struct(micros, rows, LANES, dtype=f32),
    ]
    scratch = [
        pltpu.VMEM((rows, rows), f32),
        pltpu.VMEM((rows, TILE + WIN), f32),
        pltpu.VMEM((rows + WIN, half), bf16),
        pltpu.VMEM((rows + WIN, half), bf16),
    ]
    return call(mix_kernel, micros, ins, outs, scratch, 10**10)


def prefix_gradient(ic, proj, half, dm, linear, rden, tables):
    micros = proj.shape[0]
    heads = half // HDIM
    qk = projected(proj, half)[4]
    ins = (
        [(ic, micro_spec(ic)), qk]
        + [(a, micro_spec(a)) for a in (dm, linear, rden)]
        + [(t, whole_spec(t)) for t in tables]
    )
    return call(
        prefix_grad_kernel, micros, ins, [struct(micros, heads, PHI, LANES)], [], 10**9
    )[0]


def mix_backward(ic, ir, proj, half, conv_in, tail_k, tail_v, prefix, tables, dm, linear, rden):
    micros, rows, _ = proj.shape
    width = (proj.shape[2] - 4 * half) // 2
    v, wq, wk, cg, qk = projected(proj, half)
    ins = (
        [(ic, micro_spec(ic)), (ir, micro_spec(ir)), qk, v, wq, wk, cg]
        + [(a, micro_spec(a)) for a in (conv_in, tail_k, tail_v, prefix)]
        + [(t, whole_spec(t)) for t in tables]
        + [(a, micro_spec(a)) for a in (dm, linear, rden)]
    )
    outs = [
        struct(micros, rows, width),
        struct(micros, rows, width, dtype=f32),
        struct(micros, rows, half, dtype=f32),
        struct(micros, rows, half),
        struct(micros, rows, half, dtype=f32),
        struct(micros, rows, half),
        struct(micros, rows, half),
        struct(micros, WIN, half),
        struct(micros, WIN, half),
    ]
    scratch = [
        pltpu.VMEM((rows, rows), f32),
        pltpu.VMEM((rows, TILE + WIN), f32),
        pltpu.VMEM((rows + WIN, half), bf16),
        pltpu.VMEM((rows + WIN, half), bf16),
        pltpu.VMEM((rows, width), f32),
        pltpu.VMEM((rows, width), f32),
        pltpu.VMEM((rows + WIN, HDIM), f32),
        pltpu.VMEM((rows + WIN, HDIM), f32),
    ]
    return call(mix_grad_kernel, micros, ins, outs, scratch, 2 * 10**10)


def finish_gradients(ic, proj, half, d_own, tables, dk, dv, dwk, dwq, dcg, dq, back_k, back_v):
    micros = proj.shape[0]
    v, _, _, _, qk = projected(proj, half)
    ins = (
        [(ic, micro_spec(ic)), qk, v, (d_own, micro_spec(d_own))]
        + [(t, whole_spec(t)) for t in tables]
        + [(a, micro_spec(a)) for a in (dk, dv, dwk, dwq, dcg, dq, back_k, back_v)]
    )
    return call(finish_kernel, micros, ins, [struct(*proj.shape)], [], 2 * 10**9)[0]


def cut_axis(size):
    side = max(s for s in range(1, size + 1) if s**3 <= size and size % (s * s) == 0)
    return (size // (side * side), side, side)


def strides(dims):
    return (dims[1] * dims[2], dims[2], 1)


def coords(index, dims):
    return tuple(lax.rem(lax.div(index, st), d) for st, d in zip(strides(dims), dims))


def partner(here, dims, axis, shift):
    me = sum(c * st for c, st in zip(here, strides(dims)))
    moved = lax.rem(here[axis] + shift, dims[axis])
    return me + (moved - here[axis]) * strides(dims)[axis]


def chunk_plan(widths, shares):
    total, whole = sum(share for _, share in shares), sum(widths)
    plan, done, used = [], 0, 0
    for order, share in shares:
        done += share
        end = whole if done == total else whole * done // total // LANES * LANES
        base = 0
        for w, width in enumerate(widths):
            first, last = max(used, base) - base, min(end, base + width) - base
            if last > first:
                plan.append((w, first, last, order))
            base += width
        used = end
    return plan


def transfer_script(plan, dims, depth, gather):
    queues, script, now = [[], [], []], [], 0

    def start(k, phase):
        _, first, last, order = plan[k]
        size = dims[order[phase]]
        blocks = math.prod([dims[a] for a in (order[:phase] if gather else order[phase + 1 :])])
        work = blocks * (last - first) * ((size + 1) // 2) * (size // 2) + 400
        queues[order[phase]].append([work, k, phase])
        script.append((True, k, phase))

    def fill():
        nonlocal now
        while now < len(plan) and len(queues[plan[now][3][0]]) < depth:
            start(now, 0)
            now += 1

    fill()
    while any(queues):
        step = min(queue[0][0] for queue in queues if queue)
        ended = []
        for queue in queues:
            if queue:
                queue[0][0] -= step
                if queue[0][0] <= 0:
                    ended.append(queue.pop(0))
        for _, k, phase in ended:
            script.append((False, k, phase))
            if phase < 2:
                start(k, phase + 1)
        fill()
    return script


def greet(here, dims, head):
    barrier = pltpu.get_barrier_semaphore()
    count = 0
    for axis, size in enumerate(dims):
        for shift in range(1, size):
            pl.semaphore_signal(
                barrier,
                inc=1,
                device_id=(partner(here, dims, axis, shift), head),
                device_id_type=MESH,
            )
            count += 1
    pl.semaphore_wait(barrier, count)


def gather_kernel(dims, plan, depth, count, later, *refs):
    shards, passed = refs[:count], refs[count : count + later]
    outs = refs[count + later : 2 * count + later]
    handed = refs[2 * count + later : 2 * (count + later)]
    own_sem, send, recv = refs[2 * (count + later) :]
    here = coords(lax.axis_index("seq"), dims)
    head = lax.axis_index("head")
    per_chunk = sum(d - 1 for d in dims)
    greet(here, dims, head)
    owns = [
        pltpu.make_async_copy(shards[w], outs[w].at[here], own_sem.at[w]) for w in range(count)
    ] + [pltpu.make_async_copy(passed[i], handed[i], own_sem.at[count + i]) for i in range(later)]
    started = {}

    def start(k, phase):
        w, c0, c1, order = plan[k]
        axis, known = order[phase], order[:phase]
        cols = pl.ds(c0, c1 - c0)
        index = tuple(pl.ds(0, dims[a]) if a in known else here[a] for a in range(3))
        dst = outs[w].at[index + (slice(None), cols)]
        src = shards[w].at[:, cols] if phase == 0 else dst
        at = k * per_chunk + sum(dims[a] - 1 for a in known)
        started[k, phase] = [
            pltpu.make_async_remote_copy(
                src_ref=src,
                dst_ref=dst,
                send_sem=send.at[at + shift - 1],
                recv_sem=recv.at[at + shift - 1],
                device_id=(partner(here, dims, axis, shift), head),
                device_id_type=MESH,
            )
            for shift in range(1, dims[axis])
        ]
        for copy in started[k, phase]:
            copy.start()

    for own in owns:
        own.start()
    placed = False
    for begins, k, phase in transfer_script(plan, dims, depth, True):
        if begins and phase > 0 and not placed:
            for own in owns:
                own.wait()
            placed = True
        if begins:
            start(k, phase)
        else:
            for copy in started[k, phase]:
                copy.wait_recv()
    for copies in started.values():
        for copy in copies:
            copy.wait_send()


def gather_all(shards, later, plan, dims, depth, collective_id):
    count = len(shards)
    sems = len(plan) * sum(d - 1 for d in dims)
    size = 2 * math.prod(dims) * sum(math.prod(s.shape) for s in shards)
    made = pl.pallas_call(
        functools.partial(gather_kernel, dims, plan, depth, count, len(later)),
        in_specs=[pl.BlockSpec(memory_space=pltpu.VMEM)] * (count + len(later)),
        out_specs=[pl.BlockSpec(memory_space=pl.ANY)] * (count + len(later)),
        out_shape=[jax.ShapeDtypeStruct(dims + s.shape, s.dtype) for s in shards]
        + [jax.ShapeDtypeStruct(s.shape, s.dtype) for s in later],
        scratch_shapes=[
            pltpu.SemaphoreType.DMA((count + len(later),)),
            pltpu.SemaphoreType.DMA((sems,)),
            pltpu.SemaphoreType.DMA((sems,)),
        ],
        compiler_params=pltpu.CompilerParams(
            collective_id=collective_id, has_side_effects=True, vmem_limit_bytes=VMEM_BYTES
        ),
        cost_estimate=pl.CostEstimate(flops=0, bytes_accessed=10 * size, transcendentals=0),
    )(*shards, *later)
    return made[:count], made[count:]


def scatter_kernel(dims, plan, depth, count, *refs):
    grads, outs = refs[:count], refs[count : 2 * count]
    rest = refs[2 * count :]
    n = len(plan)
    landed, sums = rest[: 3 * n], rest[3 * n : 4 * n]
    own_sem, send, recv = rest[4 * n :]
    here = coords(lax.axis_index("seq"), dims)
    head = lax.axis_index("head")
    per_chunk = sum(d - 1 for d in dims)
    greet(here, dims, head)
    started, owns = {}, {}

    def slab(order, phase, place):
        done = order[:phase]
        return tuple(
            place if a == order[phase] else (here[a] if a in done else pl.ds(0, dims[a]))
            for a in range(3)
        )

    def start(k, phase):
        w, c0, c1, order = plan[k]
        axis = order[phase]
        if phase == 0:
            owns[k] = pltpu.make_async_copy(
                grads[w].at[slab(order, 0, here[axis]) + (slice(None), pl.ds(c0, c1 - c0))],
                sums[k],
                own_sem.at[k],
            )
        made = []
        for shift in range(1, dims[axis]):
            there = lax.rem(here[axis] + shift, dims[axis])
            if phase == 0:
                src = grads[w].at[slab(order, 0, there) + (slice(None), pl.ds(c0, c1 - c0))]
            else:
                src = sums[k].at[sum_index(order, phase, there)]
            at = k * per_chunk + sum(dims[a] - 1 for a in order[:phase]) + shift - 1
            made.append(
                pltpu.make_async_remote_copy(
                    src_ref=src,
                    dst_ref=landed[3 * k + phase].at[shift - 1],
                    send_sem=send.at[at],
                    recv_sem=recv.at[at],
                    device_id=(partner(here, dims, axis, shift), head),
                    device_id_type=MESH,
                )
            )
        started[k, phase] = made
        for copy in made:
            copy.start()
        if phase == 0:
            owns[k].start()

    def sum_index(order, phase, place):
        left = [a for a in range(3) if a != order[0]]
        done = order[1:phase]
        return tuple(
            place if a == order[phase] else (here[a] if a in done else pl.ds(0, dims[a]))
            for a in left
        )

    def arrive(k, phase):
        w, c0, c1, order = plan[k]
        for copy in started[k, phase]:
            copy.wait_recv()
        if phase == 0:
            owns[k].wait()
        left = [a for a in range(3) if a not in order[: phase + 1]]
        size = math.prod([dims[a] for a in left])

        def add(b, carry):
            places, stride = {}, size
            for a in left:
                stride = stride // dims[a]
                places[a] = lax.rem(lax.div(b, stride), dims[a])
            at = tuple(places.get(a, here[a]) for a in range(3) if a != order[0])
            total = sums[k][at].astype(f32)
            for j in range(dims[order[phase]] - 1):
                arrived = landed[3 * k + phase][(j,) + tuple(places[a] for a in left)]
                total = total + arrived.astype(f32)
            if phase < 2:
                sums[k][at] = total.astype(bf16)
            else:
                outs[w][:, c0:c1] = total
            return carry

        if size == 1:
            add(0, 0)
        else:
            lax.fori_loop(0, size, add, 0)

    for begins, k, phase in transfer_script(plan, dims, depth, False):
        (start if begins else arrive)(k, phase)
    for copies in started.values():
        for copy in copies:
            copy.wait_send()


def scatter_all(grads, plan, dims, depth, collective_id):
    count = len(grads)
    sems = len(plan) * sum(d - 1 for d in dims)
    rows = grads[0].shape[3]
    landed, sums = [], []
    for _, c0, c1, order in plan:
        for phase, axis in enumerate(order):
            left = tuple(dims[a] for a in range(3) if a not in order[: phase + 1])
            landed.append(pltpu.VMEM((dims[axis] - 1,) + left + (rows, c1 - c0), bf16))
        keep = tuple(dims[a] for a in range(3) if a != order[0])
        sums.append(pltpu.VMEM(keep + (rows, c1 - c0), bf16))
    size = 2 * math.prod(dims) * sum(g.shape[3] * g.shape[4] for g in grads)
    return pl.pallas_call(
        functools.partial(scatter_kernel, dims, plan, depth, count),
        in_specs=[pl.BlockSpec(memory_space=pl.ANY)] * count,
        out_specs=[pl.BlockSpec(memory_space=pltpu.VMEM)] * count,
        out_shape=[jax.ShapeDtypeStruct(g.shape[3:], f32) for g in grads],
        scratch_shapes=landed
        + sums
        + [
            pltpu.SemaphoreType.DMA((len(plan),)),
            pltpu.SemaphoreType.DMA((sems,)),
            pltpu.SemaphoreType.DMA((sems,)),
        ],
        compiler_params=pltpu.CompilerParams(
            collective_id=collective_id, has_side_effects=True, vmem_limit_bytes=VMEM_BYTES
        ),
        cost_estimate=pl.CostEstimate(flops=0, bytes_accessed=10 * size, transcendentals=0),
    )(*grads)


def ring_pairs(dims, axis, shift):
    stride, size = strides(dims)[axis], dims[axis]
    pairs = []
    for i in range(math.prod(dims)):
        c = (i // stride) % size
        pairs.append((i, i + ((c + shift) % size - c) * stride))
    return pairs


def along(x, dims, axis, shift):
    return lax.ppermute(x, "seq", ring_pairs(dims, axis, shift))


def other_core(x):
    return lax.ppermute(x, "head", [(0, 1), (1, 0)])


def both_halves(x):
    y = other_core(x)
    first = lax.axis_index("head") == 0
    return jnp.concatenate([jnp.where(first, x, y), jnp.where(first, y, x)], axis=-1)


def core_sum(x):
    low = x.astype(bf16)
    return low.astype(f32) + other_core(low).astype(f32)


def shifted(x, by):
    size = lax.axis_size("seq")
    return lax.ppermute(x, "seq", [(i, i + by) for i in range(size) if 0 <= i + by < size])


def layout(lengths, order, positions):
    places = jnp.arange(lengths.shape[0], dtype=jnp.int32)
    picked = (order[:, None] == places[None, :]).astype(jnp.int32)
    ordered = jnp.sum(picked * lengths[None, :], axis=1, dtype=jnp.int32)
    tiles = (ordered + TILE - 1) // TILE
    first_tile = jnp.cumsum(tiles, dtype=jnp.int32) - tiles
    row_tile = positions // TILE
    after = (row_tile[:, None] >= first_tile[None, :]).astype(jnp.int32)
    slot = jnp.sum(after, axis=1, dtype=jnp.int32) - 1
    chosen = (slot[:, None] == places[None, :]).astype(jnp.int32)
    start = jnp.sum(chosen * first_tile[None, :], axis=1, dtype=jnp.int32) * TILE
    length = jnp.sum(chosen * ordered[None, :], axis=1, dtype=jnp.int32)
    return slot, start, positions - start < length


def carry_over(own, starts, rows, dims, backward):
    me = lax.axis_index("seq")
    here = coords(me, dims)

    def unbroken(a, b):
        last = lax.dynamic_index_in_dim(starts, jnp.maximum(b, 0), 1, keepdims=False)
        return (a > b) | (last < a * rows)

    def weigh(flag, x):
        return jnp.where(flag[:, None, None, None], x.astype(f32), 0.0)

    result = None
    total = own
    for axis in (2, 1, 0):
        size, stride = dims[axis], strides(dims)[axis]
        base = me // (stride * size) * (stride * size)
        c = here[axis]
        if size == 1:
            continue

        def gap(j):
            if backward:
                return unbroken(base, base + j * stride - 1)
            return unbroken(base + (j + 1) * stride, base + size * stride - 1)

        added = weigh(gap(c), total)
        for shift in range(1, size):
            j = lax.rem(c + size - shift, size)
            got = along(total, dims, axis, shift)
            if backward:
                near = (j > c) & unbroken(me + 1, base + j * stride - 1)
            else:
                near = (j < c) & unbroken(base + (j + 1) * stride, me - 1)
            part = weigh(near, got)
            result = part if result is None else result + part
            added = added + weigh(gap(j), got)
        total = added.astype(own.dtype)
    return result.astype(own.dtype)


def rsq(v):
    return lax.rsqrt(jnp.mean(v * v, axis=-1, keepdims=True) + 1e-05)


def norm_back(v, r, gain, dy):
    inner = jnp.mean(v * gain * dy, axis=-1, keepdims=True)
    return r * gain * dy - v * (r * r * r * inner), jnp.sum(dy * v * r, axis=0)


def dot_nt(a, b):
    return mul_t(a, b)


def per_device(
    layer_input,
    cotangent,
    lengths,
    doc_order,
    norm_gains,
    conv_filter,
    w_query,
    w_key,
    w_value,
    w_wquery,
    w_wkey,
    w_conv_in,
    w_conv_gate,
    w_out,
    w_gate,
    w_up,
    w_down,
):
    micros, rows, half = layer_input.shape
    dims = cut_axis(lax.axis_size("seq"))
    me = lax.axis_index("seq")
    head = lax.axis_index("head")
    place = me * rows
    tables = feature_tables(half // HDIM)
    qk = w_query.shape[1]

    small = jnp.concatenate([norm_gains, conv_filter], axis=0).T
    small = jnp.pad(small, ((0, 0), (0, LANES - small.shape[1])))
    pack_in = jnp.concatenate([w_value, w_wquery, w_wkey, w_conv_gate, w_query, w_key], axis=1)
    shards = (small, pack_in, w_conv_in, w_out.T, w_gate)
    plan = chunk_plan([s.shape[1] for s in shards], FIRST)
    fulls, later = gather_all(shards, (w_up, w_down.T), plan, dims, 3, 1)
    small_all, full_in, full_conv, full_out, full_gate = [
        full.reshape(-1, full.shape[-1]) for full in fulls
    ]
    full_up, full_down = [lax.all_gather(s, "seq", axis=0, tiled=True) for s in later]
    vectors = small_all[:, : norm_gains.shape[0] + KCONV].astype(f32).T
    gain1, gain2 = vectors[0:1], vectors[1:2]
    taps = vectors[2:]

    positions = place + jnp.arange(rows, dtype=jnp.int32)
    window_place = place - WIN + jnp.arange(WIN, dtype=jnp.int32)
    conv_place = place - (KCONV - 1) + jnp.arange(KCONV - 1, dtype=jnp.int32)
    ends = (jnp.arange(lax.axis_size("seq"), dtype=jnp.int32) + 1) * rows - 1
    info_cols, info_rows, starts, same = [], [], [], []
    for m in range(micros):
        slot, start, valid = layout(lengths[m], doc_order[m], positions)
        wslot, _, wvalid = layout(lengths[m], doc_order[m], window_place)
        cslot, _, _ = layout(lengths[m], doc_order[m], conv_place)
        starts.append(layout(lengths[m], doc_order[m], ends)[1])
        last = (slot == slot[rows - 1]) & valid
        cols = jnp.stack([slot, (start < place).astype(jnp.int32), last.astype(jnp.int32)], axis=1)
        info_cols.append(jnp.pad(cols, ((0, 0), (0, 5))))
        own = jnp.where(valid, slot, -1)
        ext = jnp.concatenate([jnp.where(wvalid, wslot, -1), own])
        ext = jnp.pad(ext, (0, WIN), constant_values=-1)
        own = jnp.pad(own, (0, 2 * WIN), constant_values=-1)
        info_rows.append(jnp.pad(jnp.stack([ext, own]), ((0, 6), (0, 0))))
        stack = jnp.concatenate([cslot, slot])
        same.append(
            jnp.stack(
                [
                    stack[KCONV - 1 - s : KCONV - 1 - s + rows] == slot
                    for s in range(1, KCONV)
                ]
            )
        )
    ic, ir, starts = jnp.stack(info_cols), jnp.stack(info_rows), jnp.stack(starts)
    same = jnp.stack(same).astype(f32)[..., None]

    x_low = both_halves(layer_input)
    cot_low = both_halves(cotangent)
    x = x_low.astype(f32)
    r1 = rsq(x)
    h1 = (x * r1 * gain1).astype(bf16)
    width = h1.shape[2]
    h1_prev = shifted(h1[:, rows - (KCONV - 1) :], 1)
    flat_h1 = h1.reshape(micros * rows, width)
    proj = mul(flat_h1, full_in).astype(bf16).reshape(micros, rows, -1)

    tail_v = shifted(proj[:, rows - WIN :, :half], 1)
    tail_k = shifted(proj[:, rows - WIN :, 2 * half : 3 * half], 1)
    own = own_states(ic, proj, half, tables)
    prefix = carry_over(own, starts, rows, dims, False)

    stacked = jnp.concatenate([h1_prev, h1], axis=1)
    h1f = h1.astype(f32)
    earlier = [
        stacked[:, KCONV - 1 - s : KCONV - 1 - s + rows].astype(f32) * same[:, s - 1]
        for s in range(1, KCONV)
    ]
    conv = taps[0] * h1f
    for s in range(1, KCONV):
        conv = conv + taps[s] * earlier[s - 1]
    conv = conv.astype(bf16)
    flat_conv = conv.reshape(micros * rows, width)
    conv_in = mul(flat_conv, full_conv).astype(bf16).reshape(micros, rows, half)

    mixed, linear, rden = mix_forward(
        ic, ir, proj, half, conv_in, tail_k, tail_v, prefix, tables
    )
    flat_mixed = mixed.reshape(micros * rows, half)
    resid = x.reshape(micros * rows, width) + core_sum(mul_t(flat_mixed, full_out))

    r2 = rsq(resid)
    h2 = (resid * r2 * gain2).astype(bf16)
    gate = mul(h2, full_gate).astype(bf16).astype(f32)
    up = mul(h2, full_up).astype(bf16).astype(f32)
    sig = 1.0 / (1.0 + jnp.exp(-gate))
    hidden = (gate * sig * up).astype(bf16)
    flat_cot = cot_low.reshape(micros * rows, width)
    grad_down = t_mul(flat_cot, hidden).astype(bf16)
    sum_down = lax.psum_scatter(grad_down, "seq", scatter_dimension=0, tiled=True).astype(f32)
    ffn = mul_t(hidden, full_down).astype(bf16)

    def pick(a, which):
        return lax.dynamic_slice_in_dim(a, which * half, half, a.ndim - 1)

    ffn_other = other_core(pick(ffn, 1 - head))
    output = pick(resid, head) + (pick(ffn, head).astype(f32) + ffn_other.astype(f32))
    output = output.astype(bf16).reshape(micros, rows, half)

    d_hidden = mul(flat_cot, full_down)
    d_gate = (d_hidden * up * (sig * (1.0 + gate * (1.0 - sig)))).astype(bf16)
    d_up = (d_hidden * (gate * sig)).astype(bf16)
    grad_gate = t_mul(h2, d_gate).astype(bf16)
    grad_up = t_mul(h2, d_up).astype(bf16)
    sum_gate = lax.psum_scatter(grad_gate, "seq", scatter_dimension=0, tiled=True).astype(f32)
    d_h2 = core_sum(mul_t(d_gate, full_gate) + mul_t(d_up, full_up))
    d_resid, d_gain2 = norm_back(resid, r2, gain2, d_h2)
    d_resid = flat_cot.astype(f32) + d_resid
    d_resid_low = d_resid.astype(bf16)

    grad_out = t_mul(d_resid_low, flat_mixed).astype(bf16)
    d_mixed = mul(d_resid_low, full_out).astype(bf16).reshape(micros, rows, half)
    d_prefix = prefix_gradient(ic, proj, half, d_mixed, linear, rden, tables)
    d_own = carry_over(d_prefix, starts, rows, dims, True)
    dq, dk, dv, dwq, dwk, dcg, dci, back_k, back_v = mix_backward(
        ic, ir, proj, half, conv_in, tail_k, tail_v, prefix, tables, d_mixed, linear, rden
    )
    back_k = shifted(back_k, -1)
    back_v = shifted(back_v, -1)
    flat_dci = dci.reshape(micros * rows, half)
    grad_conv = t_mul(flat_conv, flat_dci).astype(bf16)
    d_conv = mul_t(flat_dci, full_conv).reshape(micros, rows, width)
    d_h1 = taps[0] * d_conv
    d_taps = [jnp.sum(d_conv * h1f, axis=(0, 1))]
    before = jnp.zeros((micros, KCONV - 1, width), f32)
    for s in range(1, KCONV):
        through = d_conv * same[:, s - 1]
        d_taps.append(jnp.sum(d_conv * earlier[s - 1], axis=(0, 1)))
        moved = taps[s] * through
        d_h1 = d_h1 + jnp.pad(moved[:, s:], ((0, 0), (0, s), (0, 0)))
        before = before + jnp.pad(moved[:, :s], ((0, 0), (KCONV - 1 - s, 0), (0, 0)))
    returned = shifted(before.astype(bf16), -1).astype(f32)
    d_h1 = d_h1 + jnp.pad(returned, ((0, 0), (rows - (KCONV - 1), 0), (0, 0)))
    d_proj = finish_gradients(
        ic, proj, half, d_own, tables, dk, dv, dwk, dwq, dcg, dq, back_k, back_v
    ).reshape(micros * rows, -1)
    grad_in = t_mul(flat_h1, d_proj).astype(bf16)
    d_h1 = core_sum(d_h1.reshape(micros * rows, width) + mul_t(d_proj, full_in))
    d_x, d_gain1 = norm_back(
        x.reshape(micros * rows, width), r1.reshape(micros * rows, 1), gain1, d_h1
    )
    grad_input = pick(d_resid + d_x, head).astype(bf16).reshape(micros, rows, half)

    d_taps = jnp.stack(d_taps)
    d_taps = d_taps + other_core(d_taps)
    d_small = jnp.concatenate([d_gain1[None], d_gain2[None], d_taps], axis=0).T
    d_small = jnp.pad(d_small, ((0, 0), (0, LANES - d_small.shape[1])))
    grads = [
        g.astype(bf16).reshape(dims + (-1, g.shape[1]))
        for g in (grad_up, grad_out, grad_conv, grad_in, d_small)
    ]
    plan = [
        (w, first, last, order[::-1])
        for w, first, last, order in chunk_plan([g.shape[4] for g in grads], LAST)
    ]
    sum_up, sum_out, sum_conv, sum_in, sum_small = scatter_all(grads, plan, dims, 3, 2)
    sum_small = sum_small.T
    gains_count = norm_gains.shape[0]
    return (
        output,
        grad_input,
        sum_small[:gains_count],
        sum_small[gains_count : gains_count + KCONV],
        sum_in[:, 4 * half : 4 * half + qk],
        sum_in[:, 4 * half + qk :],
        sum_in[:, :half],
        sum_in[:, half : 2 * half],
        sum_in[:, 2 * half : 3 * half],
        sum_conv,
        sum_in[:, 3 * half : 4 * half],
        sum_out.T,
        sum_gate,
        sum_up,
        sum_down.T,
    )


def solution(mesh):
    rows_split = P(None, "seq", "head")
    vectors = P(None, "seq")
    by_rows = P("seq", "head")
    by_columns = P("head", "seq")
    weights = (by_rows,) * 7 + (by_columns, by_rows, by_rows, by_columns)
    return jax.shard_map(
        per_device,
        mesh=mesh,
        in_specs=(rows_split, rows_split, P(), P(), vectors, vectors) + weights,
        out_specs=(rows_split, rows_split, vectors, vectors) + weights,
        check_vma=False,
    )
```

```python
import functools
import math

import jax
import jax.numpy as jnp
import numpy as np
from jax import lax
from jax.experimental import pallas as pl
from jax.experimental.pallas import tpu as pltpu
from jax.sharding import PartitionSpec as P

FDIM = 16
HDIM = 112
WIN = 64
KCONV = 3
TILE = 128
LANES = 128
PHI = 160

f32 = jnp.float32
bf16 = jnp.bfloat16
VMEM_BYTES = 60 * 1024 * 1024
MESH = pl.DeviceIdType.MESH

ZYX, ZXY, XZY, YZX, XYZ, YXZ = (0, 1, 2), (0, 2, 1), (2, 0, 1), (1, 0, 2), (2, 1, 0), (1, 2, 0)
FIRST = [(ZXY, 4), (ZXY, 5), (ZYX, 3), (ZXY, 4), (YZX, 3), (ZYX, 3), (ZXY, 5), (ZYX, 5), (YXZ, 4), (XZY, 5), (ZYX, 4)]
LAST = [(ZYX, 3), (YXZ, 2), (ZXY, 4), (XZY, 2), (ZYX, 4), (ZYX, 1)]


def mul(a, b):
    return lax.dot_general(a, b, (((1,), (0,)), ((), ())), preferred_element_type=f32)


def mul_t(a, b):
    return lax.dot_general(a, b, (((1,), (1,)), ((), ())), preferred_element_type=f32)


def t_mul(a, b):
    return lax.dot_general(a, b, (((0,), (0,)), ((), ())), preferred_element_type=f32)


def feature_tables(heads):
    left = np.zeros((heads, heads * FDIM, PHI), np.float32)
    right = np.zeros((heads, heads * FDIM, PHI), np.float32)
    consts = np.zeros((8, PHI), np.float32)
    at = 0
    for a in range(FDIM):
        for b in range(a, FDIM):
            for h in range(heads):
                left[h, h * FDIM + a, at] = 0.5
                right[h, h * FDIM + b, at] = 0.5
            consts[2, at] = 1.0 / math.sqrt(2.0)
            consts[3, at] = 1.0 if a == b else 2.0
            at += 1
    for a in range(FDIM):
        for h in range(heads):
            left[h, h * FDIM + a, at] = 0.5
        consts[1, at] = 1.0
        consts[2, at] = 1.0
        consts[3, at] = 1.0
        at += 1
    consts[0, at] = consts[1, at] = consts[2, at] = consts[3, at] = 1.0
    return jnp.asarray(left, bf16), jnp.asarray(right, bf16), jnp.asarray(consts)


def with_one(values):
    rows = values.shape[0]
    lane = lax.broadcasted_iota(jnp.int32, (rows, LANES - HDIM), 1)
    extra = jnp.where(lane == 0, 1.0, 0.0).astype(values.dtype)
    return jnp.concatenate([values, extra], axis=1)


def head_cols(h):
    return slice(h * HDIM, (h + 1) * HDIM)


def features(rows, left, right, consts):
    a = mul(rows, left) + consts[0:1]
    b = mul(rows, right) + consts[1:2]
    return a, b, (a * b * consts[2:3]).astype(bf16)


def own_kernel(ic, kv, left, right, consts, state):
    half, width = split_kv(kv)
    heads = half // HDIM
    keys = kv[0, :, half + width :]
    last = ic[0, :, 2:3].astype(f32)
    table = consts[...]
    for h in range(heads):
        _, _, phi = features(keys, left[h], right[h], table)
        phi = (phi.astype(f32) * last).astype(bf16)
        state[0, h] = t_mul(phi, with_one(kv[0, :, head_cols(h)])).astype(bf16)


def linear_mask(ic, ir, t):
    rows, cols = TILE, TILE * (t + 1)
    i = lax.broadcasted_iota(jnp.int32, (rows, cols), 0) + t * TILE
    j = lax.broadcasted_iota(jnp.int32, (rows, cols), 1)
    slot = ic[0, t * TILE : (t + 1) * TILE, 0:1]
    kslot = ir[0, 1:2, 0:cols]
    return ((kslot == slot) & (j <= i)) | (j == i)


def window_mask(ic, ir, t):
    rows, cols = TILE, TILE + WIN
    i = lax.broadcasted_iota(jnp.int32, (rows, cols), 0)
    j = lax.broadcasted_iota(jnp.int32, (rows, cols), 1) - WIN
    slot = ic[0, t * TILE : (t + 1) * TILE, 0:1]
    kslot = ir[0, 0:1, t * TILE : t * TILE + cols]
    return ((kslot == slot) & (j <= i) & (i - j <= WIN)) | (j == i)


def fill_masks(ic, ir, lmask, wmask, tiles):
    for t in range(tiles):
        lmask[t * TILE : (t + 1) * TILE, 0 : TILE * (t + 1)] = jnp.where(
            linear_mask(ic, ir, t), 1.0, 0.0
        )
        wmask[t * TILE : (t + 1) * TILE, :] = jnp.where(window_mask(ic, ir, t), 0.0, -1e30)


def window_probs(wq_rows, wk_rows, mask):
    scores = mul_t(wq_rows, wk_rows) * (1.0 / math.sqrt(HDIM)) + mask
    top = jnp.max(scores, axis=1, keepdims=True)
    exponent = jnp.exp(scores - top)
    return exponent / jnp.sum(exponent, axis=1, keepdims=True)


def head_rows(rows, h):
    lane = lax.broadcasted_iota(jnp.int32, rows.shape, 1)
    return jnp.where(lane // FDIM == h, rows.astype(f32), 0.0).astype(bf16)


def window_kernel(ic, ir, kv, wq, wk, cg, ci, wkp, vp, *rest):
    part, wmask, kext, vext = rest[-4:]
    half, _ = split_kv(kv)
    rows = kv.shape[1]
    for t in range(rows // TILE):
        wmask[t * TILE : (t + 1) * TILE, :] = jnp.where(window_mask(ic, ir, t), 0.0, -1e30)
    kext[0:WIN, :] = wkp[0]
    kext[WIN:, :] = wk[0]
    vext[0:WIN, :] = vp[0]
    vext[WIN:, :] = kv[0, :, :half]
    for h in range(half // HDIM):
        hc = head_cols(h)
        vh = vext[:, hc]
        kh = kext[:, hc]
        for t in range(rows // TILE):
            r = slice(t * TILE, (t + 1) * TILE)
            e = slice(t * TILE, t * TILE + TILE + WIN)
            probs = window_probs(wq[0, r, hc], kh[e], wmask[r, :])
            conv = ci[0, r, hc].astype(f32) * cg[0, r, hc].astype(f32)
            part[0, r, hc] = mul(probs.astype(bf16), vh[e]) + conv


def linear_kernel(ic, ir, kv, part, prefix, left, right, consts, mixed, linear, rden, lmask):
    half, width = split_kv(kv)
    rows = kv.shape[1]
    for t in range(rows // TILE):
        lmask[t * TILE : (t + 1) * TILE, 0 : TILE * (t + 1)] = jnp.where(
            linear_mask(ic, ir, t), 1.0, 0.0
        )
    queries = kv[0, :, half : half + width]
    keys = kv[0, :, half + width :]
    carried = ic[0, :, 1:2].astype(f32)
    table = consts[...]
    lane = lax.broadcasted_iota(jnp.int32, (TILE, LANES), 1)
    for h in range(half // HDIM):
        hc = head_cols(h)
        vh = with_one(kv[0, :, hc])
        qh = head_rows(queries, h)
        _, _, phi = features(queries, left[h], right[h], table)
        phi = (phi.astype(f32) * (carried * table[3:4])).astype(bf16)
        for t in range(rows // TILE):
            r = slice(t * TILE, (t + 1) * TILE)
            n = TILE * (t + 1)
            a = 0.25 * mul_t(qh[r], keys[0:n])
            weight = ((1.0 + a + 0.5 * (a * a)) * lmask[r, 0:n]).astype(bf16)
            numer = mul(weight, vh[0:n]) + mul(phi[r], prefix[0, h])
            inv = 1.0 / numer[:, HDIM : HDIM + 1]
            lin = (numer * inv)[:, :HDIM]
            mixed[0, r, hc] = (lin + part[0, r, hc]).astype(bf16)
            linear[0, r, hc] = lin.astype(bf16)
            inverse = jnp.where(lane == h, inv, 0.0)
            if h == 0:
                rden[0, r, :] = inverse
            else:
                rden[0, r, :] += inverse


def d_numer(dm, linear, rden, h, r):
    hc = head_cols(h)
    inv = rden[0, r, h : h + 1]
    dn = dm[0, r, hc].astype(f32) * inv
    dd = -jnp.sum(dn * linear[0, r, hc].astype(f32), axis=1, keepdims=True)
    return dn, dd


def with_total(dn, dd):
    rows = dn.shape[0]
    high = dd.astype(bf16).astype(f32)
    lane = lax.broadcasted_iota(jnp.int32, (rows, LANES - HDIM), 1)
    extra = jnp.where(lane == 0, high, jnp.where(lane == 1, dd - high, 0.0))
    return jnp.concatenate([dn, extra], axis=1).astype(bf16)


def prefix_grad_kernel(ic, kv, dm, linear, rden, left, right, consts, d_prefix):
    half, width = split_kv(kv)
    heads = half // HDIM
    rows = dm.shape[1]
    queries = kv[0, :, half : half + width]
    carried = ic[0, :, 1:2].astype(f32)
    table = consts[...]
    for h in range(heads):
        _, _, phi = features(queries, left[h], right[h], table)
        phi = (phi.astype(f32) * (carried * table[3:4])).astype(bf16)
        dn, dd = d_numer(dm, linear, rden, h, slice(0, rows))
        d_prefix[0, h] = t_mul(phi, with_total(dn, dd)).astype(bf16)


def mix_grad_kernel(
    ic, ir, kv, wq, wk, wkp, vp, prefix, left, right, consts, dm, linear, rden, *rest
):
    dq, dk, dv, dwq, dwk, dwkp, dvp, lmask, wmask, kext, vext, dqs, dks, dvs, dwks = rest[-15:]
    half, width = split_kv(kv)
    heads = half // HDIM
    rows = kv.shape[1]
    tiles = rows // TILE
    fill_masks(ic, ir, lmask, wmask, tiles)
    queries = kv[0, :, half : half + width]
    keys = kv[0, :, half + width :]
    carried = ic[0, :, 1:2].astype(f32)
    table = consts[...]
    kext[0:WIN, :] = wkp[0]
    kext[WIN:, :] = wk[0]
    vext[0:WIN, :] = vp[0]
    vext[WIN:, :] = kv[0, :, :half]
    lane_f = lax.broadcasted_iota(jnp.int32, (PHI, LANES), 1)
    dqs[...] = jnp.zeros_like(dqs)
    dks[...] = jnp.zeros_like(dks)
    for h in range(heads):
        hc = head_cols(h)
        vh = vext[:, hc]
        kh = kext[:, hc]
        qh = head_rows(queries, h)
        khead = head_rows(keys, h)
        state = prefix[0, h].astype(f32)
        state = jnp.where(lane_f == HDIM + 1, state[:, HDIM : HDIM + 1], state).astype(bf16)
        dvs[...] = jnp.zeros_like(dvs)
        dwks[...] = jnp.zeros_like(dwks)
        for t in range(tiles):
            r = slice(t * TILE, (t + 1) * TILE)
            n = TILE * (t + 1)
            e = slice(t * TILE, t * TILE + TILE + WIN)
            dmt = dm[0, r, hc]
            probs = window_probs(wq[0, r, hc], kh[e], wmask[r, :])
            dp = mul_t(dmt, vh[e])
            ds = probs * (dp - jnp.sum(dp * probs, axis=1, keepdims=True))
            ds = (ds * (1.0 / math.sqrt(HDIM))).astype(bf16)
            dwq[0, r, hc] = mul(ds, kh[e]).astype(bf16)
            dwks[e, :] += t_mul(ds, wq[0, r, hc])
            dvs[e, :] += t_mul(probs.astype(bf16), dmt)

            dn, dd = d_numer(dm, linear, rden, h, r)
            dnb = dn.astype(bf16)
            a = 0.25 * mul_t(qh[r], keys[0:n])
            mask = lmask[r, 0:n]
            weight = ((1.0 + a + 0.5 * (a * a)) * mask).astype(bf16)
            dkern = mul_t(dnb, vh[WIN : WIN + n]) + dd
            da = (dkern * (1.0 + a) * (0.25 * mask)).astype(bf16)
            dvs[WIN : WIN + n, :] += t_mul(weight, dnb)
            dks[0:n, :] += t_mul(da, qh[r])
            g = mul_t(with_total(dn, dd), state) * (
                carried[r] * (table[2:3] * table[3:4])
            )
            fa, fb, _ = features(queries[r], left[h], right[h], table)
            dqs[r, :] += (
                mul(da, khead[0:n])
                + mul_t((g * fb).astype(bf16), left[h])
                + mul_t((g * fa).astype(bf16), right[h])
            )
        dv[0, :, hc] = dvs[WIN:, :]
        dvp[0, :, hc] = dvs[0:WIN, :].astype(bf16)
        dwk[0, :, hc] = dwks[WIN:, :]
        dwkp[0, :, hc] = dwks[0:WIN, :].astype(bf16)
    dq[0] = dqs[...].astype(bf16)
    dk[0] = dks[...]


def finish_kernel(
    ic, kv, d_own, left, right, consts, dk, dv, dwk, dwq, dcg, dq, back_k, back_v, d_kv, d_rest
):
    half, width = split_kv(kv)
    heads = half // HDIM
    rows = kv.shape[1]
    keys = kv[0, :, half + width :]
    last = ic[0, :, 2:3].astype(f32)
    table = consts[...]
    d_keys = dk[0]
    for h in range(heads):
        hc = head_cols(h)
        grad = d_own[0, h]
        fa, fb, phi = features(keys, left[h], right[h], table)
        phi = (phi.astype(f32) * last).astype(bf16)
        part = dv[0, :, hc] + mul(phi, grad)[:, :HDIM]
        d_kv[0, 0 : rows - WIN, hc] = part[0 : rows - WIN].astype(bf16)
        d_kv[0, rows - WIN :, hc] = (part[rows - WIN :] + back_v[0, :, hc].astype(f32)).astype(bf16)
        g = mul_t(with_one(kv[0, :, hc]), grad) * (last * table[2:3])
        d_keys = (
            d_keys
            + mul_t((g * fb).astype(bf16), left[h])
            + mul_t((g * fa).astype(bf16), right[h])
        )
    d_kv[0, :, half : half + width] = dq[0]
    d_kv[0, :, half + width :] = d_keys.astype(bf16)
    d_rest[0, :, 0:half] = dwq[0]
    d_rest[0, 0 : rows - WIN, half : 2 * half] = dwk[0, 0 : rows - WIN].astype(bf16)
    d_rest[0, rows - WIN :, half : 2 * half] = (
        dwk[0, rows - WIN :] + back_k[0].astype(f32)
    ).astype(bf16)
    d_rest[0, :, 2 * half :] = dcg[0]


def micro_spec(array, block=None, at=0):
    shape = array.shape
    if block is None:
        return pl.BlockSpec((1,) + shape[1:], lambda m: (m,) + (0,) * (len(shape) - 1))
    return pl.BlockSpec((1, shape[1], block), lambda m: (m, 0, at))


def whole_spec(array):
    rank = len(array.shape)
    return pl.BlockSpec(array.shape, lambda m: (0,) * rank)


def call(kernel, micros, ins, outs, scratch, flops):
    return pl.pallas_call(
        kernel,
        grid=(micros,),
        in_specs=[spec for _, spec in ins],
        out_specs=[micro_spec(o) for o in outs],
        out_shape=[jax.ShapeDtypeStruct(o.shape, o.dtype) for o in outs],
        scratch_shapes=scratch,
        compiler_params=pltpu.CompilerParams(vmem_limit_bytes=VMEM_BYTES),
        cost_estimate=pl.CostEstimate(
            flops=flops,
            bytes_accessed=sum(math.prod(o.shape) * o.dtype.itemsize for o in outs) * 3,
            transcendentals=0,
        ),
    )(*[a for a, _ in ins])


def struct(*shape, dtype=bf16):
    return jax.ShapeDtypeStruct(shape, dtype)


def parts_of(proj, half):
    return [(proj, micro_spec(proj, half, i)) for i in range(proj.shape[2] // half)]


def split_kv(kv):
    width = (kv.shape[2] - kv.shape[2] // (HDIM + 2 * FDIM) * HDIM) // 2
    half = kv.shape[2] - 2 * width
    return half, width


def micro_ins(*arrays):
    return [(a, micro_spec(a)) for a in arrays]


def table_ins(tables):
    return [(t, whole_spec(t)) for t in tables]


def awaited(arrays):
    return [(a, pl.BlockSpec(memory_space=pl.ANY)) for a in arrays]


def own_states(ic, kv, tables):
    micros = kv.shape[0]
    heads = split_kv(kv)[0] // HDIM
    ins = micro_ins(ic, kv) + table_ins(tables)
    return call(own_kernel, micros, ins, [struct(micros, heads, PHI, LANES)], [], 10**9)[0]


def window_forward(ic, ir, kv, rest, conv_in, tail_k, tail_v, after):
    micros, rows, _ = kv.shape
    half = split_kv(kv)[0]
    ins = micro_ins(ic, ir, kv) + parts_of(rest, half) + micro_ins(conv_in, tail_k, tail_v)
    scratch = [
        pltpu.VMEM((rows, TILE + WIN), f32),
        pltpu.VMEM((rows + WIN, half), bf16),
        pltpu.VMEM((rows + WIN, half), bf16),
    ]
    outs = [struct(micros, rows, half, dtype=f32)]
    return call(window_kernel, micros, ins + awaited(after), outs, scratch, 3 * 10**10)[0]


def linear_forward(ic, ir, kv, part, prefix, tables):
    micros, rows, _ = kv.shape
    half = split_kv(kv)[0]
    ins = micro_ins(ic, ir, kv, part, prefix) + table_ins(tables)
    outs = [
        struct(micros, rows, half),
        struct(micros, rows, half),
        struct(micros, rows, LANES, dtype=f32),
    ]
    return call(linear_kernel, micros, ins, outs, [pltpu.VMEM((rows, rows), f32)], 2 * 10**10)


def prefix_gradient(ic, kv, dm, linear, rden, tables):
    micros = kv.shape[0]
    heads = split_kv(kv)[0] // HDIM
    ins = micro_ins(ic, kv, dm, linear, rden) + table_ins(tables)
    outs = [struct(micros, heads, PHI, LANES)]
    return call(prefix_grad_kernel, micros, ins, outs, [], 10**9)[0]


def mix_backward(ic, ir, kv, rest, tail_k, tail_v, prefix, tables, dm, linear, rden, after):
    micros, rows, _ = kv.shape
    half, width = split_kv(kv)
    ins = (
        micro_ins(ic, ir, kv)
        + parts_of(rest, half)[:2]
        + micro_ins(tail_k, tail_v, prefix)
        + table_ins(tables)
        + micro_ins(dm, linear, rden)
        + awaited(after)
    )
    outs = [
        struct(micros, rows, width),
        struct(micros, rows, width, dtype=f32),
        struct(micros, rows, half, dtype=f32),
        struct(micros, rows, half),
        struct(micros, rows, half, dtype=f32),
        struct(micros, WIN, half),
        struct(micros, WIN, half),
    ]
    scratch = [
        pltpu.VMEM((rows, rows), f32),
        pltpu.VMEM((rows, TILE + WIN), f32),
        pltpu.VMEM((rows + WIN, half), bf16),
        pltpu.VMEM((rows + WIN, half), bf16),
        pltpu.VMEM((rows, width), f32),
        pltpu.VMEM((rows, width), f32),
        pltpu.VMEM((rows + WIN, HDIM), f32),
        pltpu.VMEM((rows + WIN, HDIM), f32),
    ]
    return call(mix_grad_kernel, micros, ins, outs, scratch, 8 * 10**10)


def finish_gradients(ic, kv, rest, d_own, tables, dk, dv, dwk, dwq, dcg, dq, back_k, back_v):
    ins = (
        micro_ins(ic, kv, d_own)
        + table_ins(tables)
        + micro_ins(dk, dv, dwk, dwq, dcg, dq, back_k, back_v)
    )
    outs = [struct(*kv.shape), struct(*rest.shape)]
    return call(finish_kernel, kv.shape[0], ins, outs, [], 2 * 10**9)


def cut_axis(size):
    side = max(s for s in range(1, size + 1) if s**3 <= size and size % (s * s) == 0)
    return (size // (side * side), side, side)


def strides(dims):
    return (dims[1] * dims[2], dims[2], 1)


def coords(index, dims):
    return tuple(lax.rem(lax.div(index, st), d) for st, d in zip(strides(dims), dims))


def partner(here, dims, axis, shift):
    me = sum(c * st for c, st in zip(here, strides(dims)))
    moved = lax.rem(here[axis] + shift, dims[axis])
    return me + (moved - here[axis]) * strides(dims)[axis]


def chunk_plan(widths, shares):
    total, whole = sum(share for _, share in shares), sum(widths)
    plan, done, used = [], 0, 0
    for order, share in shares:
        done += share
        end = whole if done == total else whole * done // total // LANES * LANES
        base = 0
        for w, width in enumerate(widths):
            first, last = max(used, base) - base, min(end, base + width) - base
            if last > first:
                plan.append((w, first, last, order))
            base += width
        used = end
    return plan


def transfer_script(plan, dims, depth, gather):
    queues, script, now = [[], [], []], [], 0

    def start(k, phase):
        _, first, last, order = plan[k]
        size = dims[order[phase]]
        blocks = math.prod([dims[a] for a in (order[:phase] if gather else order[phase + 1 :])])
        work = blocks * (last - first) * ((size + 1) // 2) * (size // 2) + 400
        queues[order[phase]].append([work, k, phase])
        script.append((True, k, phase))

    def fill():
        nonlocal now
        while now < len(plan) and len(queues[plan[now][3][0]]) < depth:
            start(now, 0)
            now += 1

    fill()
    while any(queues):
        step = min(queue[0][0] for queue in queues if queue)
        ended = []
        for queue in queues:
            if queue:
                queue[0][0] -= step
                if queue[0][0] <= 0:
                    ended.append(queue.pop(0))
        for _, k, phase in ended:
            script.append((False, k, phase))
            if phase < 2:
                start(k, phase + 1)
        fill()
    return script


def greet(here, dims, head):
    barrier = pltpu.get_barrier_semaphore()
    count = 0
    for axis, size in enumerate(dims):
        for shift in range(1, size):
            pl.semaphore_signal(
                barrier,
                inc=1,
                device_id=(partner(here, dims, axis, shift), head),
                device_id_type=MESH,
            )
            count += 1
    pl.semaphore_wait(barrier, count)


def gather_kernel(dims, plan, depth, count, later, *refs):
    shards, passed = refs[:count], refs[count : count + later]
    outs = refs[count + later : 2 * count + later]
    handed = refs[2 * count + later : 2 * (count + later)]
    own_sem, send, recv = refs[2 * (count + later) :]
    here = coords(lax.axis_index("seq"), dims)
    head = lax.axis_index("head")
    per_chunk = sum(d - 1 for d in dims)
    greet(here, dims, head)
    owns = [
        pltpu.make_async_copy(shards[w], outs[w].at[here], own_sem.at[w]) for w in range(count)
    ] + [pltpu.make_async_copy(passed[i], handed[i], own_sem.at[count + i]) for i in range(later)]
    started = {}

    def start(k, phase):
        w, c0, c1, order = plan[k]
        axis, known = order[phase], order[:phase]
        cols = pl.ds(c0, c1 - c0)
        index = tuple(pl.ds(0, dims[a]) if a in known else here[a] for a in range(3))
        dst = outs[w].at[index + (slice(None), cols)]
        src = shards[w].at[:, cols] if phase == 0 else dst
        at = k * per_chunk + sum(dims[a] - 1 for a in known)
        started[k, phase] = [
            pltpu.make_async_remote_copy(
                src_ref=src,
                dst_ref=dst,
                send_sem=send.at[at + shift - 1],
                recv_sem=recv.at[at + shift - 1],
                device_id=(partner(here, dims, axis, shift), head),
                device_id_type=MESH,
            )
            for shift in range(1, dims[axis])
        ]
        for copy in started[k, phase]:
            copy.start()

    for own in owns:
        own.start()
    placed = False
    for begins, k, phase in transfer_script(plan, dims, depth, True):
        if begins and phase > 0 and not placed:
            for own in owns:
                own.wait()
            placed = True
        if begins:
            start(k, phase)
        else:
            for copy in started[k, phase]:
                copy.wait_recv()
    for copies in started.values():
        for copy in copies:
            copy.wait_send()


def gather_all(shards, later, plan, dims, depth, collective_id):
    count = len(shards)
    sems = len(plan) * sum(d - 1 for d in dims)
    size = 2 * math.prod(dims) * sum(math.prod(s.shape) for s in shards)
    made = pl.pallas_call(
        functools.partial(gather_kernel, dims, plan, depth, count, len(later)),
        in_specs=[pl.BlockSpec(memory_space=pltpu.VMEM)] * (count + len(later)),
        out_specs=[pl.BlockSpec(memory_space=pl.ANY)] * (count + len(later)),
        out_shape=[jax.ShapeDtypeStruct(dims + s.shape, s.dtype) for s in shards]
        + [jax.ShapeDtypeStruct(s.shape, s.dtype) for s in later],
        scratch_shapes=[
            pltpu.SemaphoreType.DMA((count + len(later),)),
            pltpu.SemaphoreType.DMA((sems,)),
            pltpu.SemaphoreType.DMA((sems,)),
        ],
        compiler_params=pltpu.CompilerParams(
            collective_id=collective_id, has_side_effects=True, vmem_limit_bytes=VMEM_BYTES
        ),
        cost_estimate=pl.CostEstimate(flops=0, bytes_accessed=10 * size, transcendentals=0),
    )(*shards, *later)
    return made[:count], made[count:]


def scatter_kernel(dims, plan, depth, cuts, *refs):
    count, made = len(cuts), sum(len(c) for c in cuts)
    grads, rest = refs[:count], refs[-(made + 4 * len(plan) + 3) :]
    outs, rest = list(rest[:made]), rest[made:]
    pieces = []
    for w, widths in enumerate(cuts):
        at = 0
        for width in widths:
            pieces.append((w, at, at + width, outs[len(pieces)]))
            at += width
    n = len(plan)
    landed, sums = rest[: 3 * n], rest[3 * n : 4 * n]
    own_sem, send, recv = rest[4 * n :]
    here = coords(lax.axis_index("seq"), dims)
    head = lax.axis_index("head")
    per_chunk = sum(d - 1 for d in dims)
    greet(here, dims, head)
    started, owns = {}, {}

    def slab(order, phase, place):
        done = order[:phase]
        return tuple(
            place if a == order[phase] else (here[a] if a in done else pl.ds(0, dims[a]))
            for a in range(3)
        )

    def start(k, phase):
        w, c0, c1, order = plan[k]
        axis = order[phase]
        if phase == 0:
            owns[k] = pltpu.make_async_copy(
                grads[w].at[slab(order, 0, here[axis]) + (slice(None), pl.ds(c0, c1 - c0))],
                sums[k],
                own_sem.at[k],
            )
        made = []
        for shift in range(1, dims[axis]):
            there = lax.rem(here[axis] + shift, dims[axis])
            if phase == 0:
                src = grads[w].at[slab(order, 0, there) + (slice(None), pl.ds(c0, c1 - c0))]
            else:
                src = sums[k].at[sum_index(order, phase, there)]
            at = k * per_chunk + sum(dims[a] - 1 for a in order[:phase]) + shift - 1
            made.append(
                pltpu.make_async_remote_copy(
                    src_ref=src,
                    dst_ref=landed[3 * k + phase].at[shift - 1],
                    send_sem=send.at[at],
                    recv_sem=recv.at[at],
                    device_id=(partner(here, dims, axis, shift), head),
                    device_id_type=MESH,
                )
            )
        started[k, phase] = made
        for copy in made:
            copy.start()
        if phase == 0:
            owns[k].start()

    def sum_index(order, phase, place):
        left = [a for a in range(3) if a != order[0]]
        done = order[1:phase]
        return tuple(
            place if a == order[phase] else (here[a] if a in done else pl.ds(0, dims[a]))
            for a in left
        )

    def arrive(k, phase):
        w, c0, c1, order = plan[k]
        for copy in started[k, phase]:
            copy.wait_recv()
        if phase == 0:
            owns[k].wait()
        left = [a for a in range(3) if a not in order[: phase + 1]]
        size = math.prod([dims[a] for a in left])

        def add(b, carry):
            places, stride = {}, size
            for a in left:
                stride = stride // dims[a]
                places[a] = lax.rem(lax.div(b, stride), dims[a])
            at = tuple(places.get(a, here[a]) for a in range(3) if a != order[0])
            total = sums[k][at].astype(f32)
            for j in range(dims[order[phase]] - 1):
                arrived = landed[3 * k + phase][(j,) + tuple(places[a] for a in left)]
                total = total + arrived.astype(f32)
            if phase < 2:
                sums[k][at] = total.astype(bf16)
            else:
                for owner, first, last, out in pieces:
                    low, high = max(first, c0), min(last, c1)
                    if owner == w and low < high:
                        out[:, low - first : high - first] = total[:, low - c0 : high - c0]
            return carry

        if size == 1:
            add(0, 0)
        else:
            lax.fori_loop(0, size, add, 0)

    for begins, k, phase in transfer_script(plan, dims, depth, False):
        (start if begins else arrive)(k, phase)
    for copies in started.values():
        for copy in copies:
            copy.wait_send()


def scatter_all(grads, cuts, after, plan, dims, depth, collective_id):
    sems = len(plan) * sum(d - 1 for d in dims)
    rows = grads[0].shape[3]
    landed, sums = [], []
    for _, c0, c1, order in plan:
        for phase, axis in enumerate(order):
            left = tuple(dims[a] for a in range(3) if a not in order[: phase + 1])
            landed.append(pltpu.VMEM((dims[axis] - 1,) + left + (rows, c1 - c0), bf16))
        keep = tuple(dims[a] for a in range(3) if a != order[0])
        sums.append(pltpu.VMEM(keep + (rows, c1 - c0), bf16))
    size = 2 * math.prod(dims) * sum(g.shape[3] * g.shape[4] for g in grads)
    return pl.pallas_call(
        functools.partial(scatter_kernel, dims, plan, depth, cuts),
        in_specs=[pl.BlockSpec(memory_space=pl.ANY)] * (len(grads) + len(after)),
        out_specs=[pl.BlockSpec(memory_space=pltpu.VMEM)] * sum(len(c) for c in cuts),
        out_shape=[jax.ShapeDtypeStruct((rows, width), f32) for c in cuts for width in c],
        scratch_shapes=landed
        + sums
        + [
            pltpu.SemaphoreType.DMA((len(plan),)),
            pltpu.SemaphoreType.DMA((sems,)),
            pltpu.SemaphoreType.DMA((sems,)),
        ],
        compiler_params=pltpu.CompilerParams(
            collective_id=collective_id, has_side_effects=True, vmem_limit_bytes=VMEM_BYTES
        ),
        cost_estimate=pl.CostEstimate(flops=0, bytes_accessed=10 * size, transcendentals=0),
    )(*grads, *after)


def ring_pairs(dims, axis, shift):
    stride, size = strides(dims)[axis], dims[axis]
    pairs = []
    for i in range(math.prod(dims)):
        c = (i // stride) % size
        pairs.append((i, i + ((c + shift) % size - c) * stride))
    return pairs


def along(x, dims, axis, shift):
    return lax.ppermute(x, "seq", ring_pairs(dims, axis, shift))


def other_core(x):
    return lax.ppermute(x, "head", [(0, 1), (1, 0)])


def both_halves(x):
    y = other_core(x)
    first = lax.axis_index("head") == 0
    return jnp.concatenate([jnp.where(first, x, y), jnp.where(first, y, x)], axis=-1)


def core_sum(x):
    low = x.astype(bf16)
    return low.astype(f32) + other_core(low).astype(f32)


def shifted(x, by):
    size = lax.axis_size("seq")
    return lax.ppermute(x, "seq", [(i, i + by) for i in range(size) if 0 <= i + by < size])


def layout(lengths, order, positions):
    places = jnp.arange(lengths.shape[0], dtype=jnp.int32)
    picked = (order[:, None] == places[None, :]).astype(jnp.int32)
    ordered = jnp.sum(picked * lengths[None, :], axis=1, dtype=jnp.int32)
    tiles = (ordered + TILE - 1) // TILE
    first_tile = jnp.cumsum(tiles, dtype=jnp.int32) - tiles
    row_tile = positions // TILE
    after = (row_tile[:, None] >= first_tile[None, :]).astype(jnp.int32)
    slot = jnp.sum(after, axis=1, dtype=jnp.int32) - 1
    chosen = (slot[:, None] == places[None, :]).astype(jnp.int32)
    start = jnp.sum(chosen * first_tile[None, :], axis=1, dtype=jnp.int32) * TILE
    length = jnp.sum(chosen * ordered[None, :], axis=1, dtype=jnp.int32)
    return slot, start, positions - start < length


def gather_heads(part, dims, axis):
    size = dims[axis]
    c = coords(lax.axis_index("seq"), dims)[axis]
    pieces = [part] + [along(part, dims, axis, shift) for shift in range(1, size)]
    ordered = []
    for place in range(size):
        piece = pieces[0]
        for shift in range(1, size):
            piece = jnp.where(lax.rem(c + size - shift, size) == place, pieces[shift], piece)
        ordered.append(piece)
    return jnp.concatenate(ordered, axis=1)


def carry_over(own, starts, rows, dims, backward):
    me = lax.axis_index("seq")
    here = coords(me, dims)

    def unbroken(a, b):
        last = lax.dynamic_index_in_dim(starts, jnp.maximum(b, 0), 1, keepdims=False)
        return (a > b) | (last < a * rows)

    def weigh(flag, x):
        return jnp.where(flag[:, None, None, None], x.astype(f32), 0.0)

    result, totals = None, []
    total = own
    plane = dims[1] * dims[2]
    for axis in (2, 1, 0):
        size, stride = dims[axis], strides(dims)[axis]
        if axis == 0 and not backward and size > 1 and own.shape[1] % plane == 0:
            share = own.shape[1] // plane
            mine = lax.dynamic_slice_in_dim(total, lax.rem(me, plane) * share, share, 1)
            near = None
            for shift in range(1, size):
                j = lax.rem(here[0] + size - shift, size)
                flag = (j < here[0]) & unbroken((j + 1) * plane, here[0] * plane - 1)
                part = weigh(flag, along(mine, dims, 0, shift))
                near = part if near is None else near + part
            near = gather_heads(gather_heads(near.astype(own.dtype), dims, 2), dims, 1)
            result = result + weigh(unbroken(here[0] * plane, me - 1), near)
            continue
        base = me // (stride * size) * (stride * size)
        c = here[axis]
        if size == 1:
            continue

        def gap(j):
            if backward:
                return unbroken(base, base + j * stride - 1)
            return unbroken(base + (j + 1) * stride, base + size * stride - 1)

        added = weigh(gap(c), total)
        for shift in range(1, size):
            j = lax.rem(c + size - shift, size)
            got = along(total, dims, axis, shift)
            if backward:
                near = (j > c) & unbroken(me + 1, base + j * stride - 1)
            else:
                near = (j < c) & unbroken(base + (j + 1) * stride, me - 1)
            part = weigh(near, got)
            result = part if result is None else result + part
            added = added + weigh(gap(j), got)
        total = added.astype(own.dtype)
        totals.append(total)
    return result.astype(own.dtype), totals


def rsq(v):
    return lax.rsqrt(jnp.mean(v * v, axis=-1, keepdims=True) + 1e-05)


def norm_back(v, r, gain, dy):
    inner = jnp.mean(v * gain * dy, axis=-1, keepdims=True)
    return r * gain * dy - v * (r * r * r * inner), jnp.sum(dy * v * r, axis=0)


def dot_nt(a, b):
    return mul_t(a, b)


def per_device(
    layer_input,
    cotangent,
    lengths,
    doc_order,
    norm_gains,
    conv_filter,
    w_query,
    w_key,
    w_value,
    w_wquery,
    w_wkey,
    w_conv_in,
    w_conv_gate,
    w_out,
    w_gate,
    w_up,
    w_down,
):
    micros, rows, half = layer_input.shape
    dims = cut_axis(lax.axis_size("seq"))
    me = lax.axis_index("seq")
    head = lax.axis_index("head")
    place = me * rows
    tables = feature_tables(half // HDIM)
    qk = w_query.shape[1]

    small = jnp.concatenate([norm_gains, conv_filter], axis=0).T
    small = jnp.pad(small, ((0, 0), (0, LANES - small.shape[1])))
    pack_kv = jnp.concatenate([w_value, w_query, w_key], axis=1)
    pack_rest = jnp.concatenate([w_wquery, w_wkey, w_conv_gate], axis=1)
    shards = (small, pack_kv, pack_rest, w_conv_in, w_out.T, w_gate)
    plan = chunk_plan([s.shape[1] for s in shards], FIRST)
    fulls, later = gather_all(shards, (w_up, w_down.T), plan, dims, 3, 1)
    small_all, full_kv, full_rest, full_conv, full_out, full_gate = [
        full.reshape(-1, full.shape[-1]) for full in fulls
    ]
    full_up, full_down = [lax.all_gather(s, "seq", axis=0, tiled=True) for s in later]
    vectors = small_all[:, : norm_gains.shape[0] + KCONV].astype(f32).T
    gain1, gain2 = vectors[0:1], vectors[1:2]
    taps = vectors[2:]

    positions = place + jnp.arange(rows, dtype=jnp.int32)
    window_place = place - WIN + jnp.arange(WIN, dtype=jnp.int32)
    conv_place = place - (KCONV - 1) + jnp.arange(KCONV - 1, dtype=jnp.int32)
    ends = (jnp.arange(lax.axis_size("seq"), dtype=jnp.int32) + 1) * rows - 1
    info_cols, info_rows, starts, same = [], [], [], []
    for m in range(micros):
        slot, start, valid = layout(lengths[m], doc_order[m], positions)
        wslot, _, wvalid = layout(lengths[m], doc_order[m], window_place)
        cslot, _, _ = layout(lengths[m], doc_order[m], conv_place)
        starts.append(layout(lengths[m], doc_order[m], ends)[1])
        last = (slot == slot[rows - 1]) & valid
        cols = jnp.stack([slot, (start < place).astype(jnp.int32), last.astype(jnp.int32)], axis=1)
        info_cols.append(jnp.pad(cols, ((0, 0), (0, 5))))
        own = jnp.where(valid, slot, -1)
        ext = jnp.concatenate([jnp.where(wvalid, wslot, -1), own])
        ext = jnp.pad(ext, (0, WIN), constant_values=-1)
        own = jnp.pad(own, (0, 2 * WIN), constant_values=-1)
        info_rows.append(jnp.pad(jnp.stack([ext, own]), ((0, 6), (0, 0))))
        stack = jnp.concatenate([cslot, slot])
        same.append(
            jnp.stack(
                [
                    stack[KCONV - 1 - s : KCONV - 1 - s + rows] == slot
                    for s in range(1, KCONV)
                ]
            )
        )
    ic, ir, starts = jnp.stack(info_cols), jnp.stack(info_rows), jnp.stack(starts)
    same = jnp.stack(same).astype(f32)[..., None]

    x_low = both_halves(layer_input)
    cot_low = both_halves(cotangent)
    x = x_low.astype(f32)
    r1 = rsq(x)
    h1 = (x * r1 * gain1).astype(bf16)
    width = h1.shape[2]
    h1_prev = shifted(h1[:, rows - (KCONV - 1) :], 1)
    flat_h1 = h1.reshape(micros * rows, width)
    kv = mul(flat_h1, full_kv).astype(bf16).reshape(micros, rows, -1)
    own = own_states(ic, kv, tables)
    prefix, totals = carry_over(own, starts, rows, dims, False)
    rest = mul(flat_h1, full_rest).astype(bf16).reshape(micros, rows, -1)
    tail_v = shifted(kv[:, rows - WIN :, :half], 1)
    tail_k = shifted(rest[:, rows - WIN :, half : 2 * half], 1)

    stacked = jnp.concatenate([h1_prev, h1], axis=1)
    h1f = h1.astype(f32)
    earlier = [
        stacked[:, KCONV - 1 - s : KCONV - 1 - s + rows].astype(f32) * same[:, s - 1]
        for s in range(1, KCONV)
    ]
    conv = taps[0] * h1f
    for s in range(1, KCONV):
        conv = conv + taps[s] * earlier[s - 1]
    conv = conv.astype(bf16)
    flat_conv = conv.reshape(micros * rows, width)
    conv_in = mul(flat_conv, full_conv).astype(bf16).reshape(micros, rows, half)

    part = window_forward(ic, ir, kv, rest, conv_in, tail_k, tail_v, (totals[1],))
    mixed, linear, rden = linear_forward(ic, ir, kv, part, prefix, tables)
    flat_mixed = mixed.reshape(micros * rows, half)
    resid = x.reshape(micros * rows, width) + core_sum(mul_t(flat_mixed, full_out))

    r2 = rsq(resid)
    h2 = (resid * r2 * gain2).astype(bf16)
    gate = mul(h2, full_gate).astype(bf16).astype(f32)
    up = mul(h2, full_up).astype(bf16).astype(f32)
    sig = 1.0 / (1.0 + jnp.exp(-gate))
    hidden = (gate * sig * up).astype(bf16)
    flat_cot = cot_low.reshape(micros * rows, width)
    grad_down = t_mul(flat_cot, hidden).astype(bf16)
    sum_down = lax.psum_scatter(grad_down, "seq", scatter_dimension=0, tiled=True).astype(f32)
    ffn = mul_t(hidden, full_down).astype(bf16)

    def pick(a, which):
        return lax.dynamic_slice_in_dim(a, which * half, half, a.ndim - 1)

    ffn_other = other_core(pick(ffn, 1 - head))
    output = pick(resid, head) + (pick(ffn, head).astype(f32) + ffn_other.astype(f32))
    output = output.astype(bf16).reshape(micros, rows, half)

    d_hidden = mul(flat_cot, full_down)
    d_gate = (d_hidden * up * (sig * (1.0 + gate * (1.0 - sig)))).astype(bf16)
    d_up = (d_hidden * (gate * sig)).astype(bf16)
    grad_gate = t_mul(h2, d_gate).astype(bf16)
    grad_up = t_mul(h2, d_up).astype(bf16)
    sum_gate = lax.psum_scatter(grad_gate, "seq", scatter_dimension=0, tiled=True).astype(f32)
    d_h2 = core_sum(mul_t(d_gate, full_gate) + mul_t(d_up, full_up))
    d_resid, d_gain2 = norm_back(resid, r2, gain2, d_h2)
    d_resid = flat_cot.astype(f32) + d_resid
    d_resid_low = d_resid.astype(bf16)

    grad_out = t_mul(d_resid_low, flat_mixed).astype(bf16)
    d_mixed = mul(d_resid_low, full_out).astype(bf16).reshape(micros, rows, half)
    d_prefix = prefix_gradient(ic, kv, d_mixed, linear, rden, tables)
    d_own, totals = carry_over(d_prefix, starts, rows, dims, True)
    gate_rows = rest[:, :, 2 * half :].astype(f32)
    dm = d_mixed.astype(f32)
    dci = (dm * gate_rows).astype(bf16)
    dcg = (dm * conv_in.astype(f32)).astype(bf16)
    flat_dci = dci.reshape(micros * rows, half)
    grad_conv = t_mul(flat_conv, flat_dci).astype(bf16)
    d_conv = mul_t(flat_dci, full_conv).reshape(micros, rows, width)
    dq, dk, dv, dwq, dwk, back_k, back_v = mix_backward(
        ic, ir, kv, rest, tail_k, tail_v, prefix, tables, d_mixed, linear, rden,
        (totals[1], d_conv, grad_conv, grad_out),
    )
    back_k = shifted(back_k, -1)
    back_v = shifted(back_v, -1)
    d_h1 = taps[0] * d_conv
    d_taps = [jnp.sum(d_conv * h1f, axis=(0, 1))]
    before = jnp.zeros((micros, KCONV - 1, width), f32)
    for s in range(1, KCONV):
        through = d_conv * same[:, s - 1]
        d_taps.append(jnp.sum(d_conv * earlier[s - 1], axis=(0, 1)))
        moved = taps[s] * through
        d_h1 = d_h1 + jnp.pad(moved[:, s:], ((0, 0), (0, s), (0, 0)))
        before = before + jnp.pad(moved[:, :s], ((0, 0), (KCONV - 1 - s, 0), (0, 0)))
    returned = shifted(before.astype(bf16), -1).astype(f32)
    d_h1 = d_h1 + jnp.pad(returned, ((0, 0), (rows - (KCONV - 1), 0), (0, 0)))
    d_kv, d_rest = [
        d.reshape(micros * rows, -1)
        for d in finish_gradients(
            ic, kv, rest, d_own, tables, dk, dv, dwk, dwq, dcg, dq, back_k, back_v
        )
    ]
    grad_kv = t_mul(flat_h1, d_kv).astype(bf16)
    grad_rest = t_mul(flat_h1, d_rest).astype(bf16)
    d_h1 = d_h1.reshape(micros * rows, width) + mul_t(d_kv, full_kv) + mul_t(d_rest, full_rest)
    d_h1 = core_sum(d_h1)
    d_x, d_gain1 = norm_back(
        x.reshape(micros * rows, width), r1.reshape(micros * rows, 1), gain1, d_h1
    )
    grad_input = pick(d_resid + d_x, head).astype(bf16).reshape(micros, rows, half)

    d_taps = jnp.stack(d_taps)
    d_taps = d_taps + other_core(d_taps)
    d_small = jnp.concatenate([d_gain1[None], d_gain2[None], d_taps], axis=0).T
    d_small = jnp.pad(d_small, ((0, 0), (0, LANES - d_small.shape[1])))
    grads = [
        g.astype(bf16).reshape(dims + (-1, g.shape[1]))
        for g in (grad_up, grad_out, grad_conv, grad_rest, grad_kv, d_small)
    ]
    cuts = [[g.shape[4]] for g in grads]
    cuts[3], cuts[4] = [half] * 3, [half, qk, qk]
    plan = [
        (w, first, last, order[::-1])
        for w, first, last, order in chunk_plan([g.shape[4] for g in grads], LAST)
    ]
    sum_up, sum_out, sum_conv, s_wq, s_wk, s_cg, s_v, s_q, s_k, sum_small = scatter_all(
        grads, cuts, (sum_gate, sum_down), plan, dims, 2, 2
    )
    sum_small = sum_small.T
    gains_count = norm_gains.shape[0]
    return (
        output,
        grad_input,
        sum_small[:gains_count],
        sum_small[gains_count : gains_count + KCONV],
        s_q,
        s_k,
        s_v,
        s_wq,
        s_wk,
        sum_conv,
        s_cg,
        sum_out.T,
        sum_gate,
        sum_up,
        sum_down.T,
    )


def solution(mesh):
    rows_split = P(None, "seq", "head")
    vectors = P(None, "seq")
    by_rows = P("seq", "head")
    by_columns = P("head", "seq")
    weights = (by_rows,) * 7 + (by_columns, by_rows, by_rows, by_columns)
    return jax.shard_map(
        per_device,
        mesh=mesh,
        in_specs=(rows_split, rows_split, P(), P(), vectors, vectors) + weights,
        out_specs=(rows_split, rows_split, vectors, vectors) + weights,
        check_vma=False,
    )
```

```python
import functools
import math

import jax
import jax.numpy as jnp
import numpy as np
from jax import lax
from jax.experimental import pallas as pl
from jax.experimental.pallas import tpu as pltpu
from jax.sharding import PartitionSpec as P

FDIM = 16
HDIM = 112
WIN = 64
KCONV = 3
TILE = 128
LANES = 128
PHI = 160

f32 = jnp.float32
bf16 = jnp.bfloat16
VMEM_BYTES = 60 * 1024 * 1024
MESH = pl.DeviceIdType.MESH

ZYX, ZXY, XZY, YZX, XYZ, YXZ = (0, 1, 2), (0, 2, 1), (2, 0, 1), (1, 0, 2), (2, 1, 0), (1, 2, 0)
FIRST = [(ZXY, 4), (ZXY, 5), (ZYX, 3), (ZXY, 4), (YZX, 3), (ZYX, 3), (ZXY, 5), (ZYX, 5), (YXZ, 4), (XZY, 5), (ZYX, 4)]
LAST = [(ZYX, 3), (YXZ, 2), (ZXY, 4), (XZY, 2), (ZYX, 4), (ZYX, 1)]


def mul(a, b):
    return lax.dot_general(a, b, (((1,), (0,)), ((), ())), preferred_element_type=f32)


def mul_t(a, b):
    return lax.dot_general(a, b, (((1,), (1,)), ((), ())), preferred_element_type=f32)


def t_mul(a, b):
    return lax.dot_general(a, b, (((0,), (0,)), ((), ())), preferred_element_type=f32)


def feature_tables(heads):
    left = np.zeros((heads, heads * FDIM, PHI), np.float32)
    right = np.zeros((heads, heads * FDIM, PHI), np.float32)
    consts = np.zeros((8, PHI), np.float32)
    at = 0
    for a in range(FDIM):
        for b in range(a, FDIM):
            for h in range(heads):
                left[h, h * FDIM + a, at] = 0.5
                right[h, h * FDIM + b, at] = 0.5
            consts[2, at] = 1.0 / math.sqrt(2.0)
            consts[3, at] = 1.0 if a == b else 2.0
            at += 1
    for a in range(FDIM):
        for h in range(heads):
            left[h, h * FDIM + a, at] = 0.5
        consts[1, at] = 1.0
        consts[2, at] = 1.0
        consts[3, at] = 1.0
        at += 1
    consts[0, at] = consts[1, at] = consts[2, at] = consts[3, at] = 1.0
    return jnp.asarray(left, bf16), jnp.asarray(right, bf16), jnp.asarray(consts)


def with_one(values):
    rows = values.shape[0]
    lane = lax.broadcasted_iota(jnp.int32, (rows, LANES - HDIM), 1)
    extra = jnp.where(lane == 0, 1.0, 0.0).astype(values.dtype)
    return jnp.concatenate([values, extra], axis=1)


def head_cols(h):
    return slice(h * HDIM, (h + 1) * HDIM)


def features(rows, left, right, consts):
    a = mul(rows, left) + consts[0:1]
    b = mul(rows, right) + consts[1:2]
    return a, b, (a * b * consts[2:3]).astype(bf16)


def own_kernel(ic, kv, left, right, consts, state):
    half, width = split_kv(kv)
    heads = half // HDIM
    keys = kv[0, :, half + width :]
    last = ic[0, :, 2:3].astype(f32)
    table = consts[...]
    for h in range(heads):
        _, _, phi = features(keys, left[h], right[h], table)
        phi = (phi.astype(f32) * last).astype(bf16)
        state[0, h] = t_mul(phi, with_one(kv[0, :, head_cols(h)])).astype(bf16)


def linear_mask(ic, ir, t):
    rows, cols = TILE, TILE * (t + 1)
    i = lax.broadcasted_iota(jnp.int32, (rows, cols), 0) + t * TILE
    j = lax.broadcasted_iota(jnp.int32, (rows, cols), 1)
    slot = ic[0, t * TILE : (t + 1) * TILE, 0:1]
    kslot = ir[0, 1:2, 0:cols]
    return ((kslot == slot) & (j <= i)) | (j == i)


def window_mask(ic, ir, t):
    rows, cols = TILE, TILE + WIN
    i = lax.broadcasted_iota(jnp.int32, (rows, cols), 0)
    j = lax.broadcasted_iota(jnp.int32, (rows, cols), 1) - WIN
    slot = ic[0, t * TILE : (t + 1) * TILE, 0:1]
    kslot = ir[0, 0:1, t * TILE : t * TILE + cols]
    return ((kslot == slot) & (j <= i) & (i - j <= WIN)) | (j == i)


def fill_masks(ic, ir, lmask, wmask, tiles):
    for t in range(tiles):
        lmask[t * TILE : (t + 1) * TILE, 0 : TILE * (t + 1)] = jnp.where(
            linear_mask(ic, ir, t), 1.0, 0.0
        )
        wmask[t * TILE : (t + 1) * TILE, :] = jnp.where(window_mask(ic, ir, t), 0.0, -1e30)


def window_probs(wq_rows, wk_rows, mask):
    scores = mul_t(wq_rows, wk_rows) * (1.0 / math.sqrt(HDIM)) + mask
    top = jnp.max(scores, axis=1, keepdims=True)
    exponent = jnp.exp(scores - top)
    return exponent / jnp.sum(exponent, axis=1, keepdims=True)


def head_rows(rows, h):
    lane = lax.broadcasted_iota(jnp.int32, rows.shape, 1)
    return jnp.where(lane // FDIM == h, rows.astype(f32), 0.0).astype(bf16)


def window_kernel(ic, ir, kv, wq, wk, cg, ci, wkp, vp, *rest):
    part, wmask, kext, vext = rest[-4:]
    half, _ = split_kv(kv)
    rows = kv.shape[1]
    for t in range(rows // TILE):
        wmask[t * TILE : (t + 1) * TILE, :] = jnp.where(window_mask(ic, ir, t), 0.0, -1e30)
    kext[0:WIN, :] = wkp[0]
    kext[WIN:, :] = wk[0]
    vext[0:WIN, :] = vp[0]
    vext[WIN:, :] = kv[0, :, :half]
    for h in range(half // HDIM):
        hc = head_cols(h)
        vh = vext[:, hc]
        kh = kext[:, hc]
        for t in range(rows // TILE):
            r = slice(t * TILE, (t + 1) * TILE)
            e = slice(t * TILE, t * TILE + TILE + WIN)
            probs = window_probs(wq[0, r, hc], kh[e], wmask[r, :])
            conv = ci[0, r, hc].astype(f32) * cg[0, r, hc].astype(f32)
            part[0, r, hc] = mul(probs.astype(bf16), vh[e]) + conv


def linear_kernel(ic, ir, kv, part, prefix, left, right, consts, mixed, linear, rden, lmask):
    half, width = split_kv(kv)
    rows = kv.shape[1]
    for t in range(rows // TILE):
        lmask[t * TILE : (t + 1) * TILE, 0 : TILE * (t + 1)] = jnp.where(
            linear_mask(ic, ir, t), 1.0, 0.0
        )
    queries = kv[0, :, half : half + width]
    keys = kv[0, :, half + width :]
    carried = ic[0, :, 1:2].astype(f32)
    table = consts[...]
    lane = lax.broadcasted_iota(jnp.int32, (TILE, LANES), 1)
    for h in range(half // HDIM):
        hc = head_cols(h)
        vh = with_one(kv[0, :, hc])
        qh = head_rows(queries, h)
        _, _, phi = features(queries, left[h], right[h], table)
        phi = (phi.astype(f32) * (carried * table[3:4])).astype(bf16)
        for t in range(rows // TILE):
            r = slice(t * TILE, (t + 1) * TILE)
            n = TILE * (t + 1)
            a = 0.25 * mul_t(qh[r], keys[0:n])
            weight = ((1.0 + a + 0.5 * (a * a)) * lmask[r, 0:n]).astype(bf16)
            numer = mul(weight, vh[0:n]) + mul(phi[r], prefix[0, h])
            inv = 1.0 / numer[:, HDIM : HDIM + 1]
            lin = (numer * inv)[:, :HDIM]
            mixed[0, r, hc] = (lin + part[0, r, hc]).astype(bf16)
            linear[0, r, hc] = lin.astype(bf16)
            inverse = jnp.where(lane == h, inv, 0.0)
            if h == 0:
                rden[0, r, :] = inverse
            else:
                rden[0, r, :] += inverse


def d_numer(dm, linear, rden, h, r):
    hc = head_cols(h)
    inv = rden[0, r, h : h + 1]
    dn = dm[0, r, hc].astype(f32) * inv
    dd = -jnp.sum(dn * linear[0, r, hc].astype(f32), axis=1, keepdims=True)
    return dn, dd


def with_total(dn, dd):
    rows = dn.shape[0]
    high = dd.astype(bf16).astype(f32)
    lane = lax.broadcasted_iota(jnp.int32, (rows, LANES - HDIM), 1)
    extra = jnp.where(lane == 0, high, jnp.where(lane == 1, dd - high, 0.0))
    return jnp.concatenate([dn, extra], axis=1).astype(bf16)


def prefix_grad_kernel(ic, kv, dm, linear, rden, left, right, consts, d_prefix):
    half, width = split_kv(kv)
    heads = half // HDIM
    rows = dm.shape[1]
    queries = kv[0, :, half : half + width]
    carried = ic[0, :, 1:2].astype(f32)
    table = consts[...]
    for h in range(heads):
        _, _, phi = features(queries, left[h], right[h], table)
        phi = (phi.astype(f32) * (carried * table[3:4])).astype(bf16)
        dn, dd = d_numer(dm, linear, rden, h, slice(0, rows))
        d_prefix[0, h] = t_mul(phi, with_total(dn, dd)).astype(bf16)


def mix_grad_kernel(
    ic, ir, kv, wq, wk, wkp, vp, prefix, left, right, consts, dm, linear, rden, *rest
):
    dq, dk, dv, dwq, dwk, dwkp, dvp, lmask, wmask, kext, vext, dqs, dks, dvs, dwks = rest[-15:]
    half, width = split_kv(kv)
    heads = half // HDIM
    rows = kv.shape[1]
    tiles = rows // TILE
    fill_masks(ic, ir, lmask, wmask, tiles)
    queries = kv[0, :, half : half + width]
    keys = kv[0, :, half + width :]
    carried = ic[0, :, 1:2].astype(f32)
    table = consts[...]
    kext[0:WIN, :] = wkp[0]
    kext[WIN:, :] = wk[0]
    vext[0:WIN, :] = vp[0]
    vext[WIN:, :] = kv[0, :, :half]
    lane_f = lax.broadcasted_iota(jnp.int32, (PHI, LANES), 1)
    dqs[...] = jnp.zeros_like(dqs)
    dks[...] = jnp.zeros_like(dks)
    for h in range(heads):
        hc = head_cols(h)
        vh = vext[:, hc]
        kh = kext[:, hc]
        qh = head_rows(queries, h)
        khead = head_rows(keys, h)
        state = prefix[0, h].astype(f32)
        state = jnp.where(lane_f == HDIM + 1, state[:, HDIM : HDIM + 1], state).astype(bf16)
        dvs[...] = jnp.zeros_like(dvs)
        dwks[...] = jnp.zeros_like(dwks)
        for t in range(tiles):
            r = slice(t * TILE, (t + 1) * TILE)
            n = TILE * (t + 1)
            e = slice(t * TILE, t * TILE + TILE + WIN)
            dmt = dm[0, r, hc]
            probs = window_probs(wq[0, r, hc], kh[e], wmask[r, :])
            dp = mul_t(dmt, vh[e])
            ds = probs * (dp - jnp.sum(dp * probs, axis=1, keepdims=True))
            ds = (ds * (1.0 / math.sqrt(HDIM))).astype(bf16)
            dwq[0, r, hc] = mul(ds, kh[e]).astype(bf16)
            dwks[e, :] += t_mul(ds, wq[0, r, hc])
            dvs[e, :] += t_mul(probs.astype(bf16), dmt)

            dn, dd = d_numer(dm, linear, rden, h, r)
            dnb = dn.astype(bf16)
            a = 0.25 * mul_t(qh[r], keys[0:n])
            mask = lmask[r, 0:n]
            weight = ((1.0 + a + 0.5 * (a * a)) * mask).astype(bf16)
            dkern = mul_t(dnb, vh[WIN : WIN + n]) + dd
            da = (dkern * (1.0 + a) * (0.25 * mask)).astype(bf16)
            dvs[WIN : WIN + n, :] += t_mul(weight, dnb)
            dks[0:n, :] += t_mul(da, qh[r])
            g = mul_t(with_total(dn, dd), state) * (
                carried[r] * (table[2:3] * table[3:4])
            )
            fa, fb, _ = features(queries[r], left[h], right[h], table)
            dqs[r, :] += (
                mul(da, khead[0:n])
                + mul_t((g * fb).astype(bf16), left[h])
                + mul_t((g * fa).astype(bf16), right[h])
            )
        dv[0, :, hc] = dvs[WIN:, :]
        dvp[0, :, hc] = dvs[0:WIN, :].astype(bf16)
        dwk[0, :, hc] = dwks[WIN:, :]
        dwkp[0, :, hc] = dwks[0:WIN, :].astype(bf16)
    dq[0] = dqs[...].astype(bf16)
    dk[0] = dks[...]


def finish_kernel(
    ic, kv, d_own, left, right, consts, dk, dv, dwk, dwq, dcg, dq, back_k, back_v, d_kv, d_rest
):
    half, width = split_kv(kv)
    heads = half // HDIM
    rows = kv.shape[1]
    keys = kv[0, :, half + width :]
    last = ic[0, :, 2:3].astype(f32)
    table = consts[...]
    d_keys = dk[0]
    for h in range(heads):
        hc = head_cols(h)
        grad = d_own[0, h]
        fa, fb, phi = features(keys, left[h], right[h], table)
        phi = (phi.astype(f32) * last).astype(bf16)
        part = dv[0, :, hc] + mul(phi, grad)[:, :HDIM]
        d_kv[0, 0 : rows - WIN, hc] = part[0 : rows - WIN].astype(bf16)
        d_kv[0, rows - WIN :, hc] = (part[rows - WIN :] + back_v[0, :, hc].astype(f32)).astype(bf16)
        g = mul_t(with_one(kv[0, :, hc]), grad) * (last * table[2:3])
        d_keys = (
            d_keys
            + mul_t((g * fb).astype(bf16), left[h])
            + mul_t((g * fa).astype(bf16), right[h])
        )
    d_kv[0, :, half : half + width] = dq[0]
    d_kv[0, :, half + width :] = d_keys.astype(bf16)
    d_rest[0, :, 0:half] = dwq[0]
    d_rest[0, 0 : rows - WIN, half : 2 * half] = dwk[0, 0 : rows - WIN].astype(bf16)
    d_rest[0, rows - WIN :, half : 2 * half] = (
        dwk[0, rows - WIN :] + back_k[0].astype(f32)
    ).astype(bf16)
    d_rest[0, :, 2 * half :] = dcg[0]


def micro_spec(array, block=None, at=0):
    shape = array.shape
    if block is None:
        return pl.BlockSpec((1,) + shape[1:], lambda m: (m,) + (0,) * (len(shape) - 1))
    return pl.BlockSpec((1, shape[1], block), lambda m: (m, 0, at))


def whole_spec(array):
    rank = len(array.shape)
    return pl.BlockSpec(array.shape, lambda m: (0,) * rank)


def call(kernel, micros, ins, outs, scratch, flops):
    return pl.pallas_call(
        kernel,
        grid=(micros,),
        in_specs=[spec for _, spec in ins],
        out_specs=[micro_spec(o) for o in outs],
        out_shape=[jax.ShapeDtypeStruct(o.shape, o.dtype) for o in outs],
        scratch_shapes=scratch,
        compiler_params=pltpu.CompilerParams(vmem_limit_bytes=VMEM_BYTES),
        cost_estimate=pl.CostEstimate(
            flops=flops,
            bytes_accessed=sum(math.prod(o.shape) * o.dtype.itemsize for o in outs) * 3,
            transcendentals=0,
        ),
    )(*[a for a, _ in ins])


def struct(*shape, dtype=bf16):
    return jax.ShapeDtypeStruct(shape, dtype)


def parts_of(proj, half):
    return [(proj, micro_spec(proj, half, i)) for i in range(proj.shape[2] // half)]


def split_kv(kv):
    width = (kv.shape[2] - kv.shape[2] // (HDIM + 2 * FDIM) * HDIM) // 2
    half = kv.shape[2] - 2 * width
    return half, width


def micro_ins(*arrays):
    return [(a, micro_spec(a)) for a in arrays]


def table_ins(tables):
    return [(t, whole_spec(t)) for t in tables]


def awaited(arrays):
    return [(a, pl.BlockSpec(memory_space=pl.ANY)) for a in arrays]


def own_states(ic, kv, tables):
    micros = kv.shape[0]
    heads = split_kv(kv)[0] // HDIM
    ins = micro_ins(ic, kv) + table_ins(tables)
    return call(own_kernel, micros, ins, [struct(micros, heads, PHI, LANES)], [], 10**9)[0]


def window_forward(ic, ir, kv, rest, conv_in, tail_k, tail_v, after):
    micros, rows, _ = kv.shape
    half = split_kv(kv)[0]
    ins = micro_ins(ic, ir, kv) + parts_of(rest, half) + micro_ins(conv_in, tail_k, tail_v)
    scratch = [
        pltpu.VMEM((rows, TILE + WIN), f32),
        pltpu.VMEM((rows + WIN, half), bf16),
        pltpu.VMEM((rows + WIN, half), bf16),
    ]
    outs = [struct(micros, rows, half, dtype=f32)]
    return call(window_kernel, micros, ins + awaited(after), outs, scratch, 3 * 10**10)[0]


def linear_forward(ic, ir, kv, part, prefix, tables):
    micros, rows, _ = kv.shape
    half = split_kv(kv)[0]
    ins = micro_ins(ic, ir, kv, part, prefix) + table_ins(tables)
    outs = [
        struct(micros, rows, half),
        struct(micros, rows, half),
        struct(micros, rows, LANES, dtype=f32),
    ]
    return call(linear_kernel, micros, ins, outs, [pltpu.VMEM((rows, rows), f32)], 2 * 10**10)


def prefix_gradient(ic, kv, dm, linear, rden, tables):
    micros = kv.shape[0]
    heads = split_kv(kv)[0] // HDIM
    ins = micro_ins(ic, kv, dm, linear, rden) + table_ins(tables)
    outs = [struct(micros, heads, PHI, LANES)]
    return call(prefix_grad_kernel, micros, ins, outs, [], 10**9)[0]


def mix_backward(ic, ir, kv, rest, tail_k, tail_v, prefix, tables, dm, linear, rden, after):
    micros, rows, _ = kv.shape
    half, width = split_kv(kv)
    ins = (
        micro_ins(ic, ir, kv)
        + parts_of(rest, half)[:2]
        + micro_ins(tail_k, tail_v, prefix)
        + table_ins(tables)
        + micro_ins(dm, linear, rden)
        + awaited(after)
    )
    outs = [
        struct(micros, rows, width),
        struct(micros, rows, width, dtype=f32),
        struct(micros, rows, half, dtype=f32),
        struct(micros, rows, half),
        struct(micros, rows, half, dtype=f32),
        struct(micros, WIN, half),
        struct(micros, WIN, half),
    ]
    scratch = [
        pltpu.VMEM((rows, rows), f32),
        pltpu.VMEM((rows, TILE + WIN), f32),
        pltpu.VMEM((rows + WIN, half), bf16),
        pltpu.VMEM((rows + WIN, half), bf16),
        pltpu.VMEM((rows, width), f32),
        pltpu.VMEM((rows, width), f32),
        pltpu.VMEM((rows + WIN, HDIM), f32),
        pltpu.VMEM((rows + WIN, HDIM), f32),
    ]
    return call(mix_grad_kernel, micros, ins, outs, scratch, 8 * 10**10)


def finish_gradients(ic, kv, rest, d_own, tables, dk, dv, dwk, dwq, dcg, dq, back_k, back_v):
    ins = (
        micro_ins(ic, kv, d_own)
        + table_ins(tables)
        + micro_ins(dk, dv, dwk, dwq, dcg, dq, back_k, back_v)
    )
    outs = [struct(*kv.shape), struct(*rest.shape)]
    return call(finish_kernel, kv.shape[0], ins, outs, [], 2 * 10**9)


def cut_axis(size):
    side = max(s for s in range(1, size + 1) if s**3 <= size and size % (s * s) == 0)
    return (size // (side * side), side, side)


def strides(dims):
    return (dims[1] * dims[2], dims[2], 1)


def coords(index, dims):
    return tuple(lax.rem(lax.div(index, st), d) for st, d in zip(strides(dims), dims))


def partner(here, dims, axis, shift):
    me = sum(c * st for c, st in zip(here, strides(dims)))
    moved = lax.rem(here[axis] + shift, dims[axis])
    return me + (moved - here[axis]) * strides(dims)[axis]


def chunk_plan(widths, shares):
    total, whole = sum(share for _, share in shares), sum(widths)
    plan, done, used = [], 0, 0
    for order, share in shares:
        done += share
        end = whole if done == total else whole * done // total // LANES * LANES
        base = 0
        for w, width in enumerate(widths):
            first, last = max(used, base) - base, min(end, base + width) - base
            if last > first:
                plan.append((w, first, last, order))
            base += width
        used = end
    return plan


def transfer_script(plan, dims, depth, gather):
    queues, script, now = [[], [], []], [], 0

    def start(k, phase):
        _, first, last, order = plan[k]
        size = dims[order[phase]]
        blocks = math.prod([dims[a] for a in (order[:phase] if gather else order[phase + 1 :])])
        work = blocks * (last - first) * ((size + 1) // 2) * (size // 2) + 400
        queues[order[phase]].append([work, k, phase])
        script.append((True, k, phase))

    def fill():
        nonlocal now
        while now < len(plan) and len(queues[plan[now][3][0]]) < depth:
            start(now, 0)
            now += 1

    fill()
    while any(queues):
        step = min(queue[0][0] for queue in queues if queue)
        ended = []
        for queue in queues:
            if queue:
                queue[0][0] -= step
                if queue[0][0] <= 0:
                    ended.append(queue.pop(0))
        for _, k, phase in ended:
            script.append((False, k, phase))
            if phase < 2:
                start(k, phase + 1)
        fill()
    return script


def greet(here, dims, head):
    barrier = pltpu.get_barrier_semaphore()
    count = 0
    for axis, size in enumerate(dims):
        for shift in range(1, size):
            pl.semaphore_signal(
                barrier,
                inc=1,
                device_id=(partner(here, dims, axis, shift), head),
                device_id_type=MESH,
            )
            count += 1
    pl.semaphore_wait(barrier, count)


def gather_kernel(dims, plan, depth, count, later, *refs):
    shards, passed = refs[:count], refs[count : count + later]
    outs = refs[count + later : 2 * count + later]
    handed = refs[2 * count + later : 2 * (count + later)]
    own_sem, send, recv = refs[2 * (count + later) :]
    here = coords(lax.axis_index("seq"), dims)
    head = lax.axis_index("head")
    per_chunk = sum(d - 1 for d in dims)
    greet(here, dims, head)
    owns = [
        pltpu.make_async_copy(shards[w], outs[w].at[here], own_sem.at[w]) for w in range(count)
    ] + [pltpu.make_async_copy(passed[i], handed[i], own_sem.at[count + i]) for i in range(later)]
    started = {}

    def start(k, phase):
        w, c0, c1, order = plan[k]
        axis, known = order[phase], order[:phase]
        cols = pl.ds(c0, c1 - c0)
        index = tuple(pl.ds(0, dims[a]) if a in known else here[a] for a in range(3))
        dst = outs[w].at[index + (slice(None), cols)]
        src = shards[w].at[:, cols] if phase == 0 else dst
        at = k * per_chunk + sum(dims[a] - 1 for a in known)
        started[k, phase] = [
            pltpu.make_async_remote_copy(
                src_ref=src,
                dst_ref=dst,
                send_sem=send.at[at + shift - 1],
                recv_sem=recv.at[at + shift - 1],
                device_id=(partner(here, dims, axis, shift), head),
                device_id_type=MESH,
            )
            for shift in range(1, dims[axis])
        ]
        for copy in started[k, phase]:
            copy.start()

    for own in owns:
        own.start()
    placed = False
    for begins, k, phase in transfer_script(plan, dims, depth, True):
        if begins and phase > 0 and not placed:
            for own in owns:
                own.wait()
            placed = True
        if begins:
            start(k, phase)
        else:
            for copy in started[k, phase]:
                copy.wait_recv()
    for copies in started.values():
        for copy in copies:
            copy.wait_send()


def gather_all(shards, later, plan, dims, depth, collective_id):
    count = len(shards)
    sems = len(plan) * sum(d - 1 for d in dims)
    size = 2 * math.prod(dims) * sum(math.prod(s.shape) for s in shards)
    made = pl.pallas_call(
        functools.partial(gather_kernel, dims, plan, depth, count, len(later)),
        in_specs=[pl.BlockSpec(memory_space=pltpu.VMEM)] * (count + len(later)),
        out_specs=[pl.BlockSpec(memory_space=pl.ANY)] * (count + len(later)),
        out_shape=[jax.ShapeDtypeStruct(dims + s.shape, s.dtype) for s in shards]
        + [jax.ShapeDtypeStruct(s.shape, s.dtype) for s in later],
        scratch_shapes=[
            pltpu.SemaphoreType.DMA((count + len(later),)),
            pltpu.SemaphoreType.DMA((sems,)),
            pltpu.SemaphoreType.DMA((sems,)),
        ],
        compiler_params=pltpu.CompilerParams(
            collective_id=collective_id, has_side_effects=True, vmem_limit_bytes=VMEM_BYTES
        ),
        cost_estimate=pl.CostEstimate(flops=0, bytes_accessed=10 * size, transcendentals=0),
    )(*shards, *later)
    return made[:count], made[count:]


def scatter_kernel(dims, plan, depth, cuts, *refs):
    count = len(cuts)
    grads, rest = refs[:count], refs[-(1 + 4 * len(plan) + 3) :]
    out, rest = rest[0], rest[1:]
    starts = [sum(cuts[:w]) for w in range(count)]
    n = len(plan)
    landed, sums = rest[: 3 * n], rest[3 * n : 4 * n]
    own_sem, send, recv = rest[4 * n :]
    here = coords(lax.axis_index("seq"), dims)
    head = lax.axis_index("head")
    per_chunk = sum(d - 1 for d in dims)
    greet(here, dims, head)
    started, owns = {}, {}

    def slab(order, phase, place):
        done = order[:phase]
        return tuple(
            place if a == order[phase] else (here[a] if a in done else pl.ds(0, dims[a]))
            for a in range(3)
        )

    def start(k, phase):
        w, c0, c1, order = plan[k]
        axis = order[phase]
        if phase == 0:
            owns[k] = pltpu.make_async_copy(
                grads[w].at[slab(order, 0, here[axis]) + (slice(None), pl.ds(c0, c1 - c0))],
                sums[k],
                own_sem.at[k],
            )
        made = []
        for shift in range(1, dims[axis]):
            there = lax.rem(here[axis] + shift, dims[axis])
            if phase == 0:
                src = grads[w].at[slab(order, 0, there) + (slice(None), pl.ds(c0, c1 - c0))]
            else:
                src = sums[k].at[sum_index(order, phase, there)]
            at = k * per_chunk + sum(dims[a] - 1 for a in order[:phase]) + shift - 1
            made.append(
                pltpu.make_async_remote_copy(
                    src_ref=src,
                    dst_ref=landed[3 * k + phase].at[shift - 1],
                    send_sem=send.at[at],
                    recv_sem=recv.at[at],
                    device_id=(partner(here, dims, axis, shift), head),
                    device_id_type=MESH,
                )
            )
        started[k, phase] = made
        for copy in made:
            copy.start()
        if phase == 0:
            owns[k].start()

    def sum_index(order, phase, place):
        left = [a for a in range(3) if a != order[0]]
        done = order[1:phase]
        return tuple(
            place if a == order[phase] else (here[a] if a in done else pl.ds(0, dims[a]))
            for a in left
        )

    def arrive(k, phase):
        w, c0, c1, order = plan[k]
        for copy in started[k, phase]:
            copy.wait_recv()
        if phase == 0:
            owns[k].wait()
        left = [a for a in range(3) if a not in order[: phase + 1]]
        size = math.prod([dims[a] for a in left])

        def add(b, carry):
            places, stride = {}, size
            for a in left:
                stride = stride // dims[a]
                places[a] = lax.rem(lax.div(b, stride), dims[a])
            at = tuple(places.get(a, here[a]) for a in range(3) if a != order[0])
            total = sums[k][at].astype(f32)
            for j in range(dims[order[phase]] - 1):
                arrived = landed[3 * k + phase][(j,) + tuple(places[a] for a in left)]
                total = total + arrived.astype(f32)
            if phase < 2:
                sums[k][at] = total.astype(bf16)
            else:
                out[:, starts[w] + c0 : starts[w] + c1] = total
            return carry

        if size == 1:
            add(0, 0)
        else:
            lax.fori_loop(0, size, add, 0)

    for begins, k, phase in transfer_script(plan, dims, depth, False):
        (start if begins else arrive)(k, phase)
    for copies in started.values():
        for copy in copies:
            copy.wait_send()


def scatter_all(grads, after, plan, dims, depth, collective_id):
    cuts = [g.shape[4] for g in grads]
    sems = len(plan) * sum(d - 1 for d in dims)
    rows = grads[0].shape[3]
    landed, sums = [], []
    for _, c0, c1, order in plan:
        for phase, axis in enumerate(order):
            left = tuple(dims[a] for a in range(3) if a not in order[: phase + 1])
            landed.append(pltpu.VMEM((dims[axis] - 1,) + left + (rows, c1 - c0), bf16))
        keep = tuple(dims[a] for a in range(3) if a != order[0])
        sums.append(pltpu.VMEM(keep + (rows, c1 - c0), bf16))
    size = 2 * math.prod(dims) * sum(g.shape[3] * g.shape[4] for g in grads)
    return pl.pallas_call(
        functools.partial(scatter_kernel, dims, plan, depth, cuts),
        in_specs=[pl.BlockSpec(memory_space=pl.ANY)] * (len(grads) + len(after)),
        out_specs=pl.BlockSpec(memory_space=pltpu.VMEM),
        out_shape=jax.ShapeDtypeStruct((rows, sum(cuts)), f32),
        scratch_shapes=landed
        + sums
        + [
            pltpu.SemaphoreType.DMA((len(plan),)),
            pltpu.SemaphoreType.DMA((sems,)),
            pltpu.SemaphoreType.DMA((sems,)),
        ],
        compiler_params=pltpu.CompilerParams(
            collective_id=collective_id, has_side_effects=True, vmem_limit_bytes=VMEM_BYTES
        ),
        cost_estimate=pl.CostEstimate(flops=0, bytes_accessed=10 * size, transcendentals=0),
    )(*grads, *after)


def ring_pairs(dims, axis, shift):
    stride, size = strides(dims)[axis], dims[axis]
    pairs = []
    for i in range(math.prod(dims)):
        c = (i // stride) % size
        pairs.append((i, i + ((c + shift) % size - c) * stride))
    return pairs


def along(x, dims, axis, shift):
    return lax.ppermute(x, "seq", ring_pairs(dims, axis, shift))


def other_core(x):
    return lax.ppermute(x, "head", [(0, 1), (1, 0)])


def both_halves(x):
    y = other_core(x)
    first = lax.axis_index("head") == 0
    return jnp.concatenate([jnp.where(first, x, y), jnp.where(first, y, x)], axis=-1)


def core_sum(x):
    low = x.astype(bf16)
    return low.astype(f32) + other_core(low).astype(f32)


def shifted(x, by):
    size = lax.axis_size("seq")
    return lax.ppermute(x, "seq", [(i, i + by) for i in range(size) if 0 <= i + by < size])


def layout(lengths, order, positions):
    places = jnp.arange(lengths.shape[0], dtype=jnp.int32)
    picked = (order[:, None] == places[None, :]).astype(jnp.int32)
    ordered = jnp.sum(picked * lengths[None, :], axis=1, dtype=jnp.int32)
    tiles = (ordered + TILE - 1) // TILE
    first_tile = jnp.cumsum(tiles, dtype=jnp.int32) - tiles
    row_tile = positions // TILE
    after = (row_tile[:, None] >= first_tile[None, :]).astype(jnp.int32)
    slot = jnp.sum(after, axis=1, dtype=jnp.int32) - 1
    chosen = (slot[:, None] == places[None, :]).astype(jnp.int32)
    start = jnp.sum(chosen * first_tile[None, :], axis=1, dtype=jnp.int32) * TILE
    length = jnp.sum(chosen * ordered[None, :], axis=1, dtype=jnp.int32)
    return slot, start, positions - start < length


def gather_heads(part, dims, axis):
    size = dims[axis]
    c = coords(lax.axis_index("seq"), dims)[axis]
    pieces = [part] + [along(part, dims, axis, shift) for shift in range(1, size)]
    ordered = []
    for place in range(size):
        piece = pieces[0]
        for shift in range(1, size):
            piece = jnp.where(lax.rem(c + size - shift, size) == place, pieces[shift], piece)
        ordered.append(piece)
    return jnp.concatenate(ordered, axis=1)


def carry_over(own, starts, rows, dims, backward):
    me = lax.axis_index("seq")
    here = coords(me, dims)

    def unbroken(a, b):
        last = lax.dynamic_index_in_dim(starts, jnp.maximum(b, 0), 1, keepdims=False)
        return (a > b) | (last < a * rows)

    def weigh(flag, x):
        return jnp.where(flag[:, None, None, None], x.astype(f32), 0.0)

    result, totals = None, []
    total = own
    plane = dims[1] * dims[2]
    for axis in (2, 1, 0):
        size, stride = dims[axis], strides(dims)[axis]
        if axis == 0 and not backward and size > 1 and own.shape[1] % plane == 0:
            share = own.shape[1] // plane
            mine = lax.dynamic_slice_in_dim(total, lax.rem(me, plane) * share, share, 1)
            near = None
            for shift in range(1, size):
                j = lax.rem(here[0] + size - shift, size)
                flag = (j < here[0]) & unbroken((j + 1) * plane, here[0] * plane - 1)
                part = weigh(flag, along(mine, dims, 0, shift))
                near = part if near is None else near + part
            near = gather_heads(gather_heads(near.astype(own.dtype), dims, 2), dims, 1)
            result = result + weigh(unbroken(here[0] * plane, me - 1), near)
            continue
        base = me // (stride * size) * (stride * size)
        c = here[axis]
        if size == 1:
            continue

        def gap(j):
            if backward:
                return unbroken(base, base + j * stride - 1)
            return unbroken(base + (j + 1) * stride, base + size * stride - 1)

        added = weigh(gap(c), total)
        for shift in range(1, size):
            j = lax.rem(c + size - shift, size)
            got = along(total, dims, axis, shift)
            if backward:
                near = (j > c) & unbroken(me + 1, base + j * stride - 1)
            else:
                near = (j < c) & unbroken(base + (j + 1) * stride, me - 1)
            part = weigh(near, got)
            result = part if result is None else result + part
            added = added + weigh(gap(j), got)
        total = added.astype(own.dtype)
        totals.append(total)
    return result.astype(own.dtype), totals


def rsq(v):
    return lax.rsqrt(jnp.mean(v * v, axis=-1, keepdims=True) + 1e-05)


def norm_back(v, r, gain, dy):
    inner = jnp.mean(v * gain * dy, axis=-1, keepdims=True)
    return r * gain * dy - v * (r * r * r * inner), jnp.sum(dy * v * r, axis=0)


def dot_nt(a, b):
    return mul_t(a, b)


def per_device(
    layer_input,
    cotangent,
    lengths,
    doc_order,
    norm_gains,
    conv_filter,
    w_query,
    w_key,
    w_value,
    w_wquery,
    w_wkey,
    w_conv_in,
    w_conv_gate,
    w_out,
    w_gate,
    w_up,
    w_down,
):
    micros, rows, half = layer_input.shape
    dims = cut_axis(lax.axis_size("seq"))
    me = lax.axis_index("seq")
    head = lax.axis_index("head")
    place = me * rows
    tables = feature_tables(half // HDIM)
    qk = w_query.shape[1]

    small = jnp.concatenate([norm_gains, conv_filter], axis=0).T
    small = jnp.pad(small, ((0, 0), (0, LANES - small.shape[1])))
    pack_kv = jnp.concatenate([w_value, w_query, w_key], axis=1)
    pack_rest = jnp.concatenate([w_wquery, w_wkey, w_conv_gate], axis=1)
    shards = (small, pack_kv, pack_rest, w_conv_in, w_out.T, w_gate)
    plan = chunk_plan([s.shape[1] for s in shards], FIRST)
    fulls, later = gather_all(shards, (w_up, w_down.T), plan, dims, 3, 1)
    small_all, full_kv, full_rest, full_conv, full_out, full_gate = [
        full.reshape(-1, full.shape[-1]) for full in fulls
    ]
    full_up, full_down = [lax.all_gather(s, "seq", axis=0, tiled=True) for s in later]
    vectors = small_all[:, : norm_gains.shape[0] + KCONV].astype(f32).T
    gain1, gain2 = vectors[0:1], vectors[1:2]
    taps = vectors[2:]

    positions = place + jnp.arange(rows, dtype=jnp.int32)
    window_place = place - WIN + jnp.arange(WIN, dtype=jnp.int32)
    conv_place = place - (KCONV - 1) + jnp.arange(KCONV - 1, dtype=jnp.int32)
    ends = (jnp.arange(lax.axis_size("seq"), dtype=jnp.int32) + 1) * rows - 1
    info_cols, info_rows, starts, same = [], [], [], []
    for m in range(micros):
        slot, start, valid = layout(lengths[m], doc_order[m], positions)
        wslot, _, wvalid = layout(lengths[m], doc_order[m], window_place)
        cslot, _, _ = layout(lengths[m], doc_order[m], conv_place)
        starts.append(layout(lengths[m], doc_order[m], ends)[1])
        last = (slot == slot[rows - 1]) & valid
        cols = jnp.stack([slot, (start < place).astype(jnp.int32), last.astype(jnp.int32)], axis=1)
        info_cols.append(jnp.pad(cols, ((0, 0), (0, 5))))
        own = jnp.where(valid, slot, -1)
        ext = jnp.concatenate([jnp.where(wvalid, wslot, -1), own])
        ext = jnp.pad(ext, (0, WIN), constant_values=-1)
        own = jnp.pad(own, (0, 2 * WIN), constant_values=-1)
        info_rows.append(jnp.pad(jnp.stack([ext, own]), ((0, 6), (0, 0))))
        stack = jnp.concatenate([cslot, slot])
        same.append(
            jnp.stack(
                [
                    stack[KCONV - 1 - s : KCONV - 1 - s + rows] == slot
                    for s in range(1, KCONV)
                ]
            )
        )
    ic, ir, starts = jnp.stack(info_cols), jnp.stack(info_rows), jnp.stack(starts)
    same = jnp.stack(same).astype(f32)[..., None]

    x_low = both_halves(layer_input)
    cot_low = both_halves(cotangent)
    x = x_low.astype(f32)
    r1 = rsq(x)
    h1 = (x * r1 * gain1).astype(bf16)
    width = h1.shape[2]
    h1_prev = shifted(h1[:, rows - (KCONV - 1) :], 1)
    flat_h1 = h1.reshape(micros * rows, width)
    kv = mul(flat_h1, full_kv).astype(bf16).reshape(micros, rows, -1)
    own = own_states(ic, kv, tables)
    prefix, totals = carry_over(own, starts, rows, dims, False)
    rest = mul(flat_h1, full_rest).astype(bf16).reshape(micros, rows, -1)
    tail_v = shifted(kv[:, rows - WIN :, :half], 1)
    tail_k = shifted(rest[:, rows - WIN :, half : 2 * half], 1)

    stacked = jnp.concatenate([h1_prev, h1], axis=1)
    h1f = h1.astype(f32)
    earlier = [
        stacked[:, KCONV - 1 - s : KCONV - 1 - s + rows].astype(f32) * same[:, s - 1]
        for s in range(1, KCONV)
    ]
    conv = taps[0] * h1f
    for s in range(1, KCONV):
        conv = conv + taps[s] * earlier[s - 1]
    conv = conv.astype(bf16)
    flat_conv = conv.reshape(micros * rows, width)
    conv_in = mul(flat_conv, full_conv).astype(bf16).reshape(micros, rows, half)

    part = window_forward(ic, ir, kv, rest, conv_in, tail_k, tail_v, (totals[1],))
    mixed, linear, rden = linear_forward(ic, ir, kv, part, prefix, tables)
    flat_mixed = mixed.reshape(micros * rows, half)
    resid = x.reshape(micros * rows, width) + core_sum(mul_t(flat_mixed, full_out))

    r2 = rsq(resid)
    h2 = (resid * r2 * gain2).astype(bf16)
    gate = mul(h2, full_gate).astype(bf16).astype(f32)
    up = mul(h2, full_up).astype(bf16).astype(f32)
    sig = 1.0 / (1.0 + jnp.exp(-gate))
    hidden = (gate * sig * up).astype(bf16)
    flat_cot = cot_low.reshape(micros * rows, width)
    grad_down = t_mul(flat_cot, hidden).astype(bf16)
    sum_down = lax.psum_scatter(grad_down, "seq", scatter_dimension=0, tiled=True).astype(f32)
    ffn = mul_t(hidden, full_down).astype(bf16)

    def pick(a, which):
        return lax.dynamic_slice_in_dim(a, which * half, half, a.ndim - 1)

    ffn_other = other_core(pick(ffn, 1 - head))
    output = pick(resid, head) + (pick(ffn, head).astype(f32) + ffn_other.astype(f32))
    output = output.astype(bf16).reshape(micros, rows, half)

    d_hidden = mul(flat_cot, full_down)
    d_gate = (d_hidden * up * (sig * (1.0 + gate * (1.0 - sig)))).astype(bf16)
    d_up = (d_hidden * (gate * sig)).astype(bf16)
    grad_gate = t_mul(h2, d_gate).astype(bf16)
    grad_up = t_mul(h2, d_up).astype(bf16)
    sum_gate = lax.psum_scatter(grad_gate, "seq", scatter_dimension=0, tiled=True).astype(f32)
    d_h2 = core_sum(mul_t(d_gate, full_gate) + mul_t(d_up, full_up))
    d_resid, d_gain2 = norm_back(resid, r2, gain2, d_h2)
    d_resid = flat_cot.astype(f32) + d_resid
    d_resid_low = d_resid.astype(bf16)

    grad_out = t_mul(d_resid_low, flat_mixed).astype(bf16)
    d_mixed = mul(d_resid_low, full_out).astype(bf16).reshape(micros, rows, half)
    d_prefix = prefix_gradient(ic, kv, d_mixed, linear, rden, tables)
    d_own, totals = carry_over(d_prefix, starts, rows, dims, True)
    gate_rows = rest[:, :, 2 * half :].astype(f32)
    dm = d_mixed.astype(f32)
    dci = (dm * gate_rows).astype(bf16)
    dcg = (dm * conv_in.astype(f32)).astype(bf16)
    flat_dci = dci.reshape(micros * rows, half)
    grad_conv = t_mul(flat_conv, flat_dci).astype(bf16)
    d_conv = mul_t(flat_dci, full_conv).reshape(micros, rows, width)
    dq, dk, dv, dwq, dwk, back_k, back_v = mix_backward(
        ic, ir, kv, rest, tail_k, tail_v, prefix, tables, d_mixed, linear, rden,
        (totals[1], d_conv, grad_conv, grad_out),
    )
    back_k = shifted(back_k, -1)
    back_v = shifted(back_v, -1)
    d_h1 = taps[0] * d_conv
    d_taps = [jnp.sum(d_conv * h1f, axis=(0, 1))]
    before = jnp.zeros((micros, KCONV - 1, width), f32)
    for s in range(1, KCONV):
        through = d_conv * same[:, s - 1]
        d_taps.append(jnp.sum(d_conv * earlier[s - 1], axis=(0, 1)))
        moved = taps[s] * through
        d_h1 = d_h1 + jnp.pad(moved[:, s:], ((0, 0), (0, s), (0, 0)))
        before = before + jnp.pad(moved[:, :s], ((0, 0), (KCONV - 1 - s, 0), (0, 0)))
    returned = shifted(before.astype(bf16), -1).astype(f32)
    d_h1 = d_h1 + jnp.pad(returned, ((0, 0), (rows - (KCONV - 1), 0), (0, 0)))
    d_kv, d_rest = [
        d.reshape(micros * rows, -1)
        for d in finish_gradients(
            ic, kv, rest, d_own, tables, dk, dv, dwk, dwq, dcg, dq, back_k, back_v
        )
    ]
    grad_kv = t_mul(flat_h1, d_kv).astype(bf16)
    grad_rest = t_mul(flat_h1, d_rest).astype(bf16)
    d_h1 = d_h1.reshape(micros * rows, width) + mul_t(d_kv, full_kv) + mul_t(d_rest, full_rest)
    d_h1 = core_sum(d_h1)
    d_x, d_gain1 = norm_back(
        x.reshape(micros * rows, width), r1.reshape(micros * rows, 1), gain1, d_h1
    )
    grad_input = pick(d_resid + d_x, head).astype(bf16).reshape(micros, rows, half)

    d_taps = jnp.stack(d_taps)
    d_taps = d_taps + other_core(d_taps)
    d_small = jnp.concatenate([d_gain1[None], d_gain2[None], d_taps], axis=0).T
    d_small = jnp.pad(d_small, ((0, 0), (0, LANES - d_small.shape[1])))
    grads = [
        g.astype(bf16).reshape(dims + (-1, g.shape[1]))
        for g in (grad_up, grad_out, grad_conv, grad_rest, grad_kv, d_small)
    ]
    plan = [
        (w, first, last, order[::-1])
        for w, first, last, order in chunk_plan([g.shape[4] for g in grads], LAST)
    ]
    sums = scatter_all(grads, (sum_gate, sum_down), plan, dims, 2, 2)
    ff = w_up.shape[1]
    widths = (ff, half, half, half, half, half, half, qk, qk, LANES)
    ends = [sum(widths[: i + 1]) for i in range(len(widths))]
    sum_up, sum_out, sum_conv, s_wq, s_wk, s_cg, s_v, s_q, s_k, sum_small = [
        sums[:, end - size : end] for end, size in zip(ends, widths)
    ]
    sum_small = sum_small.T
    gains_count = norm_gains.shape[0]
    return (
        output,
        grad_input,
        sum_small[:gains_count],
        sum_small[gains_count : gains_count + KCONV],
        s_q,
        s_k,
        s_v,
        s_wq,
        s_wk,
        sum_conv,
        s_cg,
        sum_out.T,
        sum_gate,
        sum_up,
        sum_down.T,
    )


def solution(mesh):
    rows_split = P(None, "seq", "head")
    vectors = P(None, "seq")
    by_rows = P("seq", "head")
    by_columns = P("head", "seq")
    weights = (by_rows,) * 7 + (by_columns, by_rows, by_rows, by_columns)
    return jax.shard_map(
        per_device,
        mesh=mesh,
        in_specs=(rows_split, rows_split, P(), P(), vectors, vectors) + weights,
        out_specs=(rows_split, rows_split, vectors, vectors) + weights,
        check_vma=False,
    )
```
